128 devices in a mesh: band: 32 (over x, z, core), dom: 4 (over y).
Axes of the slice: x: 4, y: 4, z: 4, core: 2. Of those that a mesh axis runs over, the one named last changes fastest.
Arguments:
- grid_inputs: bfloat16 [131072, 474], P(('band', 'dom')), may hold values from -6 to 6
- mesh_latent: bfloat16 [32768, 512], P(('band', 'dom')), may hold values from -6 to 6
- edge_state: bfloat16 [262144, 512], P(('band', 'dom')), may hold values from -6 to 6
- cotangent: bfloat16 [131072, 227], P(('band', 'dom')), may hold values from -0.15625 to 0.15625
- w_embed: bfloat16 [474, 512], replicated, may hold values from -0.25 to 0.25
- w_send: bfloat16 [512, 512], replicated, may hold values from -0.25 to 0.25
- w_recv: bfloat16 [512, 512], replicated, may hold values from -0.25 to 0.25
- w_edge: bfloat16 [1536, 512], replicated, may hold values from -0.15625 to 0.15625
- w_mesh_out: bfloat16 [512, 512], replicated, may hold values from -0.25 to 0.25
- w_grid_out: bfloat16 [512, 512], replicated, may hold values from -0.25 to 0.25
- w_predict: bfloat16 [512, 227], replicated, may hold values from -0.25 to 0.25
- enc_owner: int32 [131072, 1], P(('band', 'dom')), may hold values from 0 to 127; in each aligned block of 1024 rows (0 to 1023, 1024 to 2047, ...) at most 24 rows name the same one
- enc_local: int32 [131072], P(('band', 'dom')), may hold values from 0 to 255
- halo_rows: int32 [128, 128, 8], P(('band', 'dom')), may hold values from 0 to 255
- edge_src_dev: int32 [262144], P(('band', 'dom')), may hold values from 0 to 127
- edge_src_slot: int32 [262144], P(('band', 'dom')), may hold values from 0 to 7
- edge_dst: int32 [262144], P(('band', 'dom')), may hold values from 0 to 255
Outputs:
- prediction: bfloat16 [131072, 227], P(('band', 'dom'))
- grad_edge: float32 [1536, 512], P('band', 'dom')
The draws below stay inside these ranges and needn't reach their ends.
Inputs may be any that keep to these rules, and one draw needn't show every extreme that they name: `enc_owner`: in the 1024 rows of one device no device index appears more than 24 times, and some index appears exactly 24 times.
All inputs are finite; a program needn't handle non-finite values.
Results may differ from the reference program's by a relative error of at most 0.015.
Values may be sent and summed in bfloat16 or wider, within the bound.
A program may use at most 128 MiB of HBM per device.

```python
import math
import jax
import jax.numpy as jnp
import numpy as np
from jax import lax

D = 512
IN = 227
IN_X = 474
G = 1024
M = 256
E = 2048
SHARDS = 128
CAP = 24
HCAP = 8
NG = 131072
NM = 32768
NE = 262144


def with_ends(values, own_key, low, top_value):
    index_at = [jax.random.randint(jax.random.fold_in(own_key, axis), (), 0, length) for axis, length in enumerate(values.shape)]
    longest = values.shape.index(max(values.shape))
    next_to = index_at[:longest] + [(index_at[longest] + 1) % values.shape[longest]] + index_at[longest + 1:]
    return values.at[tuple(index_at)].set(low).at[tuple(next_to)].set(top_value)


def shard_levels(own_key, extent, shards, smallest, high):
    def one(dim, shards_of):
        heights = jax.random.uniform(jax.random.fold_in(jax.random.fold_in(own_key, 6), dim), (shards_of,), jnp.float32, smallest / len(shards), high / len(shards))
        return jnp.repeat(jnp.exp(heights), extent[dim] // shards_of).reshape((-1,) + (1,) * (len(extent) - dim - 1))

    gain = one(*shards[0])
    for cut in shards[1:]:
        gain = gain * one(*cut)
    return gain


def assign_block(key, own, number, rows, number_of, top, bound, lean):
    sequence = jax.random.permutation(key, number_of)
    crowded, usual = portions_of(number_of, rows * top, bound, lean, True), portions_of(number_of, rows * top, bound, lean, False)
    places = jnp.arange(number_of)

    def named(tallies, rotation):
        used = int((tallies > 0).sum())
        fixed = max(1, used // 4)
        moved = fixed + (places - fixed + rotation * (used - fixed)) % max(1, number_of - fixed)
        return jnp.zeros((number_of,), jnp.int32).at[sequence[jnp.where(places < fixed, places, moved)]].set(jnp.asarray(tallies, jnp.int32))

    tallies = jnp.where(number % 4 == 0, named(crowded, number // 4), named(usual, number - number // 4 - 1))
    mixed = jax.random.permutation(jax.random.fold_in(own, 3), number_of)
    source_of, sink = mixed[0:number_of // 2 * 2:2], mixed[1:number_of // 2 * 2:2]
    slack = jnp.minimum(tallies[source_of] - 1, bound - tallies[sink]) // 2
    slack = jnp.where((source_of == sequence[0]) | (sink == sequence[0]) | (tallies[sink] == 0), 0, jnp.maximum(slack, 0))
    moved = jax.random.randint(jax.random.fold_in(own, 4), (number_of // 2,), 0, 1 << 20) % (slack + 1)
    tallies = tallies.at[source_of].add(-moved).at[sink].add(moved)
    labels = jnp.searchsorted(jnp.cumsum(tallies), jnp.arange(rows * top), side="right").astype(jnp.int32)
    table = labels.reshape(top, rows).T
    table = table[jax.random.permutation(jax.random.fold_in(own, 1), rows)]
    rotation = jax.random.randint(jax.random.fold_in(own, 2), (rows, 1), 0, top)
    return jnp.take_along_axis(table, (jnp.arange(top)[None, :] + rotation) % top, axis=1)


def portions_of(amount, total, reach, lean, full):
    portions = [(1 << 20) // math.isqrt(standing ** lean) + 1 for standing in range(1, amount + 1)]
    largest = reach if full else min(reach, max(-(-total // amount), total * portions[0] // sum(portions)))
    least = 1 if total - largest >= amount - 1 else 0
    given, rest = [largest] + [least] * (amount - 1), total - largest - least * (amount - 1)
    while rest > 0:
        candidates = [i for i in range(1, amount) if given[i] < largest] or [i for i in range(1, amount) if given[i] < reach]
        mass, remaining = sum([portions[i] for i in candidates]), rest
        for i in candidates:
            extra = min(reach - given[i], max(1, remaining * portions[i] // mass), rest)
            given[i] = given[i] + extra
            rest = rest - extra
    return np.array(given)


def gaussian(own_key, extent, deviation, most, shards=(), kind=jnp.bfloat16):
    entries = deviation * jax.random.normal(own_key, extent, jnp.float32)
    if shards:
        entries = entries * shard_levels(own_key, extent, shards, -0.22, 0.18)
    return jnp.clip(entries, -most, most).astype(kind)


def setup_inputs(seed: int = 0) -> dict:
    seeds = jax.random.split(jax.random.key(seed), 18)
    grid_inputs = gaussian(seeds[0], (NG, IN_X), 1.0, 6.0, ((0, 128),))
    mesh_latent = gaussian(seeds[1], (NM, D), 1.0, 6.0, ((0, 128),))
    edge_state = gaussian(seeds[2], (NE, D), 1.0, 6.0, ((0, 128),))
    cotangent = gaussian(seeds[3], (NG, IN), ((G * SHARDS) ** -0.5 * 4), 0.15625, ((0, 128),))
    w_embed = gaussian(seeds[4], (IN_X, D), IN_X ** -0.5, 0.25)
    w_send = gaussian(seeds[5], (D, D), D ** -0.5, 0.25)
    w_recv = gaussian(seeds[6], (D, D), D ** -0.5, 0.25)
    w_edge = gaussian(seeds[7], (3 * D, D), (3 * D) ** -0.5, 0.15625)
    w_mesh_out = gaussian(seeds[8], (D, D), D ** -0.5, 0.25)
    w_grid_out = gaussian(seeds[9], (D, D), D ** -0.5, 0.25)
    w_predict = gaussian(seeds[10], (D, IN), D ** -0.5, 0.25)
    enc_owner_keys = jax.random.split(jax.random.fold_in(seeds[11], 1), NG // G)
    enc_owner_turns = jax.random.permutation(jax.random.fold_in(seeds[11], 3), NG // G)
    enc_owner = jax.vmap(lambda own, number: assign_block(jax.random.fold_in(seeds[11], 2), own, number, G, SHARDS, 1, CAP, 1))(enc_owner_keys, enc_owner_turns).reshape((NG, 1))
    enc_local = with_ends(jax.random.randint(seeds[12], (NG,), 0, M), jax.random.fold_in(seeds[12], 1), 0, M - 1).astype(jnp.int32)
    halo_rows = with_ends(jax.random.randint(seeds[13], (SHARDS, SHARDS, HCAP), 0, M), jax.random.fold_in(seeds[13], 1), 0, M - 1).astype(jnp.int32)
    edge_src_dev = with_ends(jax.random.randint(seeds[14], (NE,), 0, SHARDS), jax.random.fold_in(seeds[14], 1), 0, SHARDS - 1).astype(jnp.int32)
    edge_src_slot = with_ends(jax.random.randint(seeds[15], (NE,), 0, HCAP), jax.random.fold_in(seeds[15], 1), 0, HCAP - 1).astype(jnp.int32)
    edge_dst = with_ends(jax.random.randint(seeds[16], (NE,), 0, M), jax.random.fold_in(seeds[16], 1), 0, M - 1).astype(jnp.int32)
    return dict(grid_inputs=grid_inputs, mesh_latent=mesh_latent, edge_state=edge_state, cotangent=cotangent, w_embed=w_embed, w_send=w_send, w_recv=w_recv, w_edge=w_edge, w_mesh_out=w_mesh_out, w_grid_out=w_grid_out, w_predict=w_predict, enc_owner=enc_owner, enc_local=enc_local, halo_rows=halo_rows, edge_src_dev=edge_src_dev, edge_src_slot=edge_src_slot, edge_dst=edge_dst)


def swish(value):
    return value * jax.nn.sigmoid(value)

def norm_rows(values):
    center = values - lax.optimization_barrier(jnp.mean(values, axis=-1, keepdims=True))
    spread = lax.optimization_barrier(jnp.mean(center * center, axis=-1, keepdims=True))
    return center * lax.rsqrt(spread + 1e-05)

def reference(grid_inputs, mesh_latent, edge_state, cotangent, w_embed, w_send, w_recv, w_edge, w_mesh_out, w_grid_out, w_predict, enc_owner, enc_local, halo_rows, edge_src_dev, edge_src_slot, edge_dst):
    total_nodes = M * SHARDS
    query = jnp.dot(mesh_latent, w_recv, preferred_element_type=jnp.float32)
    grid_x = grid_inputs.reshape(SHARDS, G, IN_X)
    grid_cot = cotangent.reshape(SHARDS, G, IN)
    targets = (enc_owner[:, 0] * M + enc_local).astype(jnp.int32).reshape(SHARDS, G)

    def embed(block):
        return swish(jnp.dot(block, w_embed, preferred_element_type=jnp.float32)).astype(jnp.bfloat16)

    def encode(carry, pair):
        block, target = pair
        hidden = embed(block)
        proj = jnp.dot(hidden, w_send, preferred_element_type=jnp.float32).astype(jnp.bfloat16)
        message = swish(proj.astype(jnp.float32) + jnp.take(query, target, axis=0))
        return (carry + jax.ops.segment_sum(message, target, total_nodes), None)
    agg, _ = lax.scan(encode, jnp.zeros((total_nodes, D), jnp.float32), (grid_x, targets))
    encoded = (mesh_latent.astype(jnp.float32) + norm_rows(agg)).astype(jnp.bfloat16)
    shard_ids = jnp.arange(SHARDS, dtype=jnp.int32)
    src_dev = edge_src_dev.reshape(SHARDS, E)
    src_slot = edge_src_slot.reshape(SHARDS, E)
    dst_local = edge_dst.reshape(SHARDS, E)
    states = edge_state.reshape(SHARDS, E, D)

    def edge_inputs(shard, devs, slots, dsts, state):
        local_rows = halo_rows[devs, shard, slots]
        senders = jnp.take(encoded, (devs * M + local_rows).astype(jnp.int32), axis=0)
        mine = lax.dynamic_slice_in_dim(encoded, (shard * M).astype(jnp.int32), M, 0)
        receivers = jnp.take(mine, dsts, axis=0)
        joined = jnp.concatenate([state, senders, receivers], axis=1)
        pre = jnp.dot(joined, w_edge, preferred_element_type=jnp.float32)
        edge_sum = jax.ops.segment_sum(swish(pre), dsts, M)
        return (joined, pre, mine, edge_sum)

    def process(args):
        joined, pre, mine, edge_sum = edge_inputs(*args)
        return (mine.astype(jnp.float32) + norm_rows(edge_sum)).astype(jnp.bfloat16)
    updated = lax.map(process, (shard_ids, src_dev, src_slot, dst_local, states)).reshape(total_nodes, D)

    def decode(carry, args):
        block, target, cot = args
        hidden = embed(block)
        read = jnp.take(updated, target, axis=0)
        zed = jnp.dot(read, w_mesh_out, preferred_element_type=jnp.float32) + jnp.dot(hidden, w_grid_out, preferred_element_type=jnp.float32)
        act = swish(zed).astype(jnp.bfloat16)
        pred = jnp.dot(act, w_predict, preferred_element_type=jnp.float32).astype(jnp.bfloat16)
        d_act = jnp.dot(cot, w_predict.T, preferred_element_type=jnp.float32)
        _, swish_back = jax.vjp(swish, zed)
        d_zed = swish_back(d_act)[0].astype(jnp.bfloat16)
        d_read = jnp.dot(d_zed, w_mesh_out.T, preferred_element_type=jnp.float32).astype(jnp.bfloat16)
        return (carry + jax.ops.segment_sum(d_read.astype(jnp.float32), target, total_nodes), pred)
    d_updated, preds = lax.scan(decode, jnp.zeros((total_nodes, D), jnp.float32), (grid_x, targets, grid_cot))

    def backward(carry, args):
        shard, devs, slots, dsts, state = args
        joined, pre, mine, edge_sum = edge_inputs(shard, devs, slots, dsts, state)
        d_mine = lax.dynamic_slice_in_dim(d_updated, (shard * M).astype(jnp.int32), M, 0)
        _, norm_back = jax.vjp(norm_rows, edge_sum)
        d_sum = norm_back(d_mine)[0]
        d_edge = jnp.take(d_sum, dsts, axis=0)
        _, swish_back = jax.vjp(swish, pre)
        d_pre = swish_back(d_edge)[0].astype(jnp.bfloat16)
        term = lax.dot_general(joined, d_pre, (((0,), (0,)), ((), ())), preferred_element_type=jnp.float32)
        return (carry + term, None)
    grad_edge, _ = lax.scan(backward, jnp.zeros((3 * D, D), jnp.float32), (shard_ids, src_dev, src_slot, dst_local, states))
    return (preds.reshape(SHARDS * G, IN), grad_edge)
```

```python
import functools

import jax
import jax.numpy as jnp
from jax import lax
from jax.experimental import pallas as pl
from jax.experimental.pallas import tpu as pltpu
from jax.sharding import PartitionSpec as P

MESH = pl.DeviceIdType.MESH
F32 = jnp.float32
BF16 = jnp.bfloat16
CHUNKS = 8
STRIDE = 53
STRIDE_INVERSE = 29


def sigmoid(value):
    return 0.5 * jnp.tanh(0.5 * value) + 0.5


def dot(a, b):
    return jnp.dot(a, b, preferred_element_type=F32)


def one_hot(mask):
    return jnp.where(mask, 1.0, 0.0).astype(BF16)


def iota(shape, dim):
    return lax.broadcasted_iota(jnp.int32, shape, dim)


def column(row):
    wide = jnp.broadcast_to(row.astype(F32), (8, row.shape[1]))
    return jnp.transpose(wide)[:, :1].astype(jnp.int32)


def moments(values):
    center = values - jnp.mean(values, axis=-1, keepdims=True)
    spread = jnp.mean(center * center, axis=-1, keepdims=True)
    scale = lax.rsqrt(spread + 1e-05)
    return center * scale, scale


def fold(values, parts, depth):
    half = values.shape[1] // 2
    cut = values.reshape(parts, depth, 2 * half)
    return jnp.concatenate([cut[:, :, :half], cut[:, :, half:]], axis=1).astype(BF16)


def unfold(values):
    parts, twice, half = values.shape
    depth = twice // 2
    wide = values.astype(F32)
    return jnp.concatenate([wide[:, :depth], wide[:, depth:]], axis=2).reshape(parts * depth, 2 * half)


def kernel(
    nx,
    nz,
    ny,
    cap,
    halo,
    x_ref,
    ml_ref,
    es_ref,
    cot_ref,
    wemb_ref,
    wsend_ref,
    wrecv_ref,
    wedge_ref,
    wm_ref,
    wg_ref,
    wp_ref,
    owner_ref,
    local_ref,
    halo_ref,
    dev_ref,
    slot_ref,
    dst_ref,
    pred_ref,
    grad_ref,
    xs,
    cs,
    web,
    wpp,
    wpt,
    slots,
    sbuf,
    rbuf,
    csbuf,
    crbuf,
    obuf,
    inbuf,
    bsend,
    bland,
    hbuf,
    own,
    ownt,
    query,
    agg,
    enc,
    hal,
    osnd,
    orcv,
    orcvt,
    part,
    est,
    inb,
    snd,
    esum,
    mesh_part,
    dz,
    dsum,
    dpre,
    gland,
    g2,
    gl2,
    pick,
    a_send,
    a_recv,
    c_send,
    c_recv,
    h_send,
    h_recv,
    b_send,
    b_recv,
    p_send,
    p_recv,
    g_send,
    g_recv,
):
    n = nx * nz * 2 * ny
    chips = nx * nz * ny
    grid, width_in = x_ref.shape
    nodes, width = ml_ref.shape
    edges = es_ref.shape[0]
    outs = cot_ref.shape[1]
    spc = n // CHUNKS
    rows = spc * cap
    epc = edges // CHUNKS
    band, y = lax.axis_index("band"), lax.axis_index("dom")
    x, z, k = band // (2 * nz), (band // 2) % nz, band % 2
    me = band * ny + y

    def shift(r, sign):
        q = (r * STRIDE) % n
        dy, dk, dz_, dx = q % ny, (q // ny) % 2, (q // (2 * ny)) % nz, q // (2 * ny * nz)
        tx = (x + sign * dx + nx) % nx
        tz = (z + sign * dz_ + nz) % nz
        tk = (k + dk) % 2
        ty = (y + sign * dy + ny) % ny
        return (tx * nz + tz) * 2 + tk, ty

    barrier = pltpu.get_barrier_semaphore()

    def greet(r, carry):
        tb, ty = shift(r, 1)
        pl.semaphore_signal(barrier, inc=1, device_id=(tb, ty), device_id_type=MESH)
        return carry

    lax.fori_loop(1, n, greet, 0)

    o = owner_ref[...]
    member = jnp.where(o == iota((n, grid), 0), 1.0, 0.0)
    tri = min(128, grid)
    before = one_hot(iota((tri, tri), 0) < iota((tri, tri), 1))
    base = jnp.zeros((n, 1), F32)
    ranks = []
    for i in range(grid // tri):
        m = member[:, i * tri : (i + 1) * tri]
        count = dot(m.astype(BF16), before) + base
        ranks.append(jnp.sum(count * m, axis=0, keepdims=True))
        base = base + jnp.sum(m, axis=1, keepdims=True)
    rank = jnp.concatenate(ranks, axis=1).astype(jnp.int32)
    ly, lz = ny.bit_length() - 1, nz.bit_length() - 1
    qy = ((o & (ny - 1)) - y) & (ny - 1)
    qk = ((o >> ly) - k) & 1
    qz = ((o >> (ly + 1)) - z) & (nz - 1)
    qx = ((o >> (ly + 1 + lz)) - x) & (nx - 1)
    q = ((qx * nz + qz) * 2 + qk) * ny + qy
    slots[...] = ((q * STRIDE_INVERSE) & (n - 1)) * cap + rank

    xs[...] = jnp.zeros_like(xs)
    xs[:, :width_in] = x_ref[...]
    tail = xs[:, width - 128 :].astype(F32)
    mark = iota((grid, 128), 1) == width_in - (width - 128)
    xs[:, width - 128 :] = jnp.where(mark, (column(local_ref[...]) + 1).astype(F32), tail).astype(BF16)
    cs[...] = jnp.zeros_like(cs)
    cs[:, :outs] = cot_ref[...]

    pl.semaphore_wait(barrier, n - 1)

    def send(src, dst, send_sem, recv_sem, to):
        pltpu.make_async_remote_copy(
            src_ref=src, dst_ref=dst, send_sem=send_sem, recv_sem=recv_sem, device_id=to, device_id_type=MESH
        ).start()

    def take(ref, sem):
        pltpu.make_async_copy(ref, ref, sem).wait()

    def send_parts(c, src, dst, send_sem, recv_sem, sign):
        def one(i, carry):
            r = c * spc + i

            @pl.when(r > 0)
            def _():
                send(src.at[r], dst.at[r], send_sem, recv_sem.at[c], shift(r, sign))

            return carry

        lax.fori_loop(0, spc, one, 0)

        @pl.when(c == 0)
        def _():
            pltpu.make_async_copy(src.at[0], dst.at[0], recv_sem.at[0]).start()

    def pack(c, carry):
        place = one_hot(slots[...] == iota((rows, grid), 0) + c * rows)
        sbuf[pl.ds(c * spc, spc)] = fold(dot(place, xs[...]), spc, cap)
        send_parts(c, sbuf, rbuf, a_send, a_recv, 1)
        csbuf[pl.ds(c * spc, spc)] = fold(dot(place, cs[...]), spc, cap)
        return carry

    lax.fori_loop(0, CHUNKS, pack, 0)

    web[...] = jnp.zeros_like(web)
    web[:width_in, :] = wemb_ref[...]
    wpp[...] = jnp.zeros_like(wpp)
    wpp[:, :outs] = wp_ref[...]
    wpt[...] = jnp.transpose(wpp[...])
    query[...] = dot(ml_ref[...], wrecv_ref[...]).astype(BF16)

    def encode(c, carry):
        take(rbuf.at[pl.ds(c * spc, spc)], a_recv.at[c])
        wide = unfold(rbuf[pl.ds(c * spc, spc)])
        mark = iota((rows, 128), 1) == width_in - (width - 128)
        label = jnp.sum(jnp.where(mark, wide[:, width - 128 :], 0.0), axis=1, keepdims=True)
        hit = one_hot(label.astype(jnp.int32) - 1 == iota((rows, nodes), 1))
        lines = pl.ds(pl.multiple_of(c * rows, rows), rows)
        own[lines, :] = hit
        hit_t = jnp.transpose(hit)
        ownt[:, lines] = hit_t
        hid = dot(wide.astype(BF16), web[...])
        hid = (hid * sigmoid(hid)).astype(BF16)
        hbuf[lines, :] = hid
        arg = dot(hid, wsend_ref[...]) + dot(hit, query[...])
        agg[...] += dot(hit_t, (arg * sigmoid(arg)).astype(BF16))
        return carry

    def prepare(c, carry):
        lines = pl.ds(pl.multiple_of(c * epc, epc), epc)
        dst = dst_ref[:, lines]
        orcvt[:, lines] = one_hot(dst == iota((nodes, epc), 0))
        orcv[lines, :] = one_hot(column(dst) == iota((epc, nodes), 1))
        source = column(dev_ref[:, lines] * halo + slot_ref[:, lines])
        osnd[lines, :] = one_hot(source == iota((epc, n * halo), 1))
        state = es_ref[lines, :]
        est[:, lines] = jnp.transpose(state)
        part[lines, :] = dot(state, wedge_ref[:width, :])
        hpc = n * halo // CHUNKS
        spots = pl.ds(pl.multiple_of(c * hpc, hpc), hpc)
        hal[spots, :] = one_hot(column(halo_ref[:, spots]) == iota((hpc, nodes), 1))
        gpc = grid // CHUNKS
        spots = pl.ds(pl.multiple_of(c * gpc, gpc), gpc)
        pick[spots, :] = one_hot(column(slots[:, spots]) == iota((gpc, n * cap), 1))
        return carry

    lax.fori_loop(0, CHUNKS, prepare, 0)
    agg[...] = jnp.zeros_like(agg)
    lax.fori_loop(0, CHUNKS, encode, 0)

    encoded = (ml_ref[...].astype(F32) + moments(agg[...])[0]).astype(BF16)
    enc[...] = encoded

    def outbound(c, carry):
        hpc = n * halo // CHUNKS
        spots = pl.ds(pl.multiple_of(c * hpc, hpc), hpc)
        obuf[pl.ds(c * spc, spc)] = fold(dot(hal[spots, :], enc[...]), spc, halo)
        return carry

    lax.fori_loop(0, CHUNKS, outbound, 0)

    def send_halo(r, carry):
        tb, ty = shift(r, 1)
        send(obuf.at[tb * ny + ty], inbuf.at[me], h_send, h_recv, (tb, ty))
        return carry

    lax.fori_loop(1, n, send_halo, 0)
    pltpu.make_async_copy(obuf.at[me], inbuf.at[me], h_recv).start()

    def send_cot(c, carry):
        send_parts(c, csbuf, crbuf, c_send, c_recv, 1)
        return carry

    lax.fori_loop(0, CHUNKS, send_cot, 0)

    own_part = dot(enc[...], wedge_ref[2 * width :, :]).astype(BF16)
    mesh_part[...] = own_part

    def edge_own(c, carry):
        lines = pl.ds(pl.multiple_of(c * epc, epc), epc)
        part[lines, :] += dot(orcv[lines, :], mesh_part[...])
        return carry

    lax.fori_loop(0, CHUNKS, edge_own, 0)
    esum[...] = jnp.zeros_like(esum)
    take(inbuf, h_recv)
    inb[...] = unfold(inbuf[...]).astype(BF16)

    def edge_forward(c, carry):
        lines = pl.ds(pl.multiple_of(c * epc, epc), epc)
        sender = dot(osnd[lines, :], inb[...]).astype(BF16)
        snd[lines, :] = sender
        pre = part[lines, :] + dot(sender, wedge_ref[width : 2 * width, :])
        part[lines, :] = pre
        esum[...] += dot(orcvt[:, lines], (pre * sigmoid(pre)).astype(BF16))
        return carry

    lax.fori_loop(0, CHUNKS, edge_forward, 0)
    normed, scale = moments(esum[...])
    updated = (enc[...].astype(F32) + normed).astype(BF16)
    mesh_part[...] = dot(updated, wm_ref[...]).astype(BF16)
    dz[...] = jnp.zeros_like(dz)

    def decode(c, carry):
        lines = pl.ds(pl.multiple_of(c * rows, rows), rows)
        zed = dot(hbuf[lines, :], wg_ref[...]) + dot(own[lines, :], mesh_part[...])
        sig = sigmoid(zed)
        bsend[pl.ds(c * spc, spc)] = fold(dot((zed * sig).astype(BF16), wpp[...]), spc, cap)

        def one(i, inner):
            r = c * spc + i

            @pl.when(r > 0)
            def _():
                send(bsend.at[r], bland.at[r], b_send, b_recv, shift(r, -1))

            return inner

        lax.fori_loop(0, spc, one, 0)
        take(crbuf.at[pl.ds(c * spc, spc)], c_recv.at[c])
        slope = dot(unfold(crbuf[pl.ds(c * spc, spc)]).astype(BF16), wpt[...])
        slope = (slope * sig * (1.0 + zed * (1.0 - sig))).astype(BF16)
        dz[...] += dot(ownt[:, lines], slope)
        return carry

    lax.fori_loop(0, CHUNKS, decode, 0)
    pltpu.make_async_copy(bsend.at[0], bland.at[0], b_recv).start()

    slope = lax.dot_general(
        dz[...].astype(BF16), wm_ref[...], (((1,), (1,)), ((), ())), preferred_element_type=F32
    )
    normed, scale = moments(esum[...])
    slope = scale * (
        slope
        - jnp.mean(slope, axis=-1, keepdims=True)
        - normed * jnp.mean(slope * normed, axis=-1, keepdims=True)
    )
    dsum[...] = slope.astype(BF16)

    def edge_backward(c, carry):
        lines = pl.ds(pl.multiple_of(c * epc, epc), epc)
        pre = part[lines, :]
        sig = sigmoid(pre)
        slope = dot(orcv[lines, :], dsum[...])
        dpre[lines, :] = (slope * sig * (1.0 + pre * (1.0 - sig))).astype(BF16)
        return carry

    lax.fori_loop(0, CHUNKS, edge_backward, 0)
    hbuf[:width, :] = dot(est[...], dpre[...]).astype(BF16)
    hbuf[width : 2 * width, :] = lax.dot_general(
        snd[...], dpre[...], (((0,), (0,)), ((), ())), preferred_element_type=F32
    ).astype(BF16)
    received = dot(orcvt[...], dpre[...]).astype(BF16)
    hbuf[2 * width : 3 * width, :] = lax.dot_general(
        enc[...], received, (((0,), (0,)), ((), ())), preferred_element_type=F32
    ).astype(BF16)

    share = 3 * width // (nx * nz * 2)

    def send_pair(i, carry):
        block = pl.ds(pl.multiple_of((i * 2 + 1 - k) * share, 16), share)
        send(hbuf.at[block, :], gland.at[i], p_send, p_recv, ((x * nz + z) * 2 + 1 - k, y))
        return carry

    lax.fori_loop(0, nx * nz, send_pair, 0)
    take(gland, p_recv)
    cols = width // ny

    def add_pair(i, carry):
        block = pl.ds(pl.multiple_of((i * 2 + k) * share, 16), share)
        both = (hbuf[block, :].astype(F32) + gland[i].astype(F32)).astype(BF16)
        for d in range(ny):
            g2[i * ny + d] = both[:, d * cols : (d + 1) * cols]
        return carry

    lax.fori_loop(0, nx * nz, add_pair, 0)
    chip = (x * nz + z) * ny + y

    def send_grad(r, carry):
        q = (r * STRIDE) % chips
        ty = (y + q % ny) % ny
        tz = (z + (q // ny) % nz) % nz
        tx = (x + q // (ny * nz)) % nx
        xz = tx * nz + tz
        send(g2.at[xz * ny + ty], gl2.at[chip], g_send, g_recv, (xz * 2 + k, ty))
        return carry

    lax.fori_loop(1, chips, send_grad, 0)
    pltpu.make_async_copy(g2.at[chip], gl2.at[chip], g_recv).start()

    take(bland, b_recv)

    def arrange(c, carry):
        lines = pl.ds(pl.multiple_of(c * rows, rows), rows)
        own[lines, :] = unfold(bland[pl.ds(c * spc, spc)]).astype(BF16)
        return carry

    lax.fori_loop(0, CHUNKS, arrange, 0)

    def choose(c, carry):
        gpc = grid // CHUNKS
        spots = pl.ds(pl.multiple_of(c * gpc, gpc), gpc)
        pred_ref[spots, :] = dot(pick[spots, :], own[...])[:, :outs].astype(BF16)
        return carry

    lax.fori_loop(0, CHUNKS, choose, 0)
    take(gl2, g_recv)
    grad_ref[...] = jnp.zeros_like(grad_ref)

    def add_grad(i, carry):
        grad_ref[...] += gl2[i].astype(F32)
        return carry

    lax.fori_loop(0, chips, add_grad, 0)
    take(sbuf.at[pl.ds(1, n - 1)], a_send)
    take(csbuf.at[pl.ds(1, n - 1)], c_send)
    take(obuf.at[pl.ds(1, n - 1)], h_send)
    take(bsend.at[pl.ds(1, n - 1)], b_send)
    take(gland, p_send)
    take(g2.at[pl.ds(1, chips - 1)], g_send)


def body(
    grid_inputs,
    mesh_latent,
    edge_state,
    cotangent,
    w_embed,
    w_send,
    w_recv,
    w_edge,
    w_mesh_out,
    w_grid_out,
    w_predict,
    enc_owner,
    enc_local,
    halo_rows,
    edge_src_dev,
    edge_src_slot,
    edge_dst,
    bands,
    doms,
):
    side = int(round((bands // 2) ** 0.5))
    n = bands * doms
    chips = n // 2
    grid = grid_inputs.shape[0]
    nodes, width = mesh_latent.shape
    edges = edge_state.shape[0]
    outs = cotangent.shape[1]
    wide_out = 256
    cap = 3 * grid // n
    halo = halo_rows.shape[2]
    share, cols = 3 * width // bands, width // doms
    vmem = pltpu.VMEM
    scratch = [
        vmem((grid, width), BF16),
        vmem((grid, wide_out), BF16),
        vmem((width, width), BF16),
        vmem((width, wide_out), BF16),
        vmem((wide_out, width), BF16),
        vmem((1, grid), jnp.int32),
        vmem((n, 2 * cap, width // 2), BF16),
        vmem((n, 2 * cap, width // 2), BF16),
        vmem((n, 2 * cap, wide_out // 2), BF16),
        vmem((n, 2 * cap, wide_out // 2), BF16),
        vmem((n, 2 * halo, width // 2), BF16),
        vmem((n, 2 * halo, width // 2), BF16),
        vmem((n, 2 * cap, wide_out // 2), BF16),
        vmem((n, 2 * cap, wide_out // 2), BF16),
        vmem((max(n * cap, 3 * width), width), BF16),
        vmem((n * cap, nodes), BF16),
        vmem((nodes, n * cap), BF16),
        vmem((nodes, width), BF16),
        vmem((nodes, width), F32),
        vmem((nodes, width), BF16),
        vmem((n * halo, nodes), BF16),
        vmem((edges, n * halo), BF16),
        vmem((edges, nodes), BF16),
        vmem((nodes, edges), BF16),
        vmem((edges, width), F32),
        vmem((width, edges), BF16),
        vmem((n * halo, width), BF16),
        vmem((edges, width), BF16),
        vmem((nodes, width), F32),
        vmem((nodes, width), BF16),
        vmem((nodes, width), F32),
        vmem((nodes, width), BF16),
        vmem((edges, width), BF16),
        vmem((bands // 2, share, width), BF16),
        vmem((chips, share, cols), BF16),
        vmem((chips, share, cols), BF16),
        vmem((grid, n * cap), BF16),
    ]
    dma = pltpu.SemaphoreType.DMA
    for _ in range(2):
        scratch += [dma, dma((CHUNKS,))]
    scratch += [dma] * 8
    return pl.pallas_call(
        functools.partial(kernel, side, side, doms, cap, halo),
        out_shape=(
            jax.ShapeDtypeStruct((grid, outs), BF16),
            jax.ShapeDtypeStruct((share, cols), F32),
        ),
        in_specs=[pl.BlockSpec(memory_space=vmem)] * 17,
        out_specs=(pl.BlockSpec(memory_space=vmem),) * 2,
        scratch_shapes=scratch,
        compiler_params=pltpu.CompilerParams(
            collective_id=0, has_side_effects=True, vmem_limit_bytes=63 * 1024 * 1024
        ),
        cost_estimate=pl.CostEstimate(flops=25 * 10**9, bytes_accessed=10**7, transcendentals=10**7),
    )(
        grid_inputs,
        mesh_latent,
        edge_state,
        cotangent,
        w_embed,
        w_send,
        w_recv,
        w_edge,
        w_mesh_out,
        w_grid_out,
        w_predict,
        enc_owner.reshape(1, grid),
        enc_local.reshape(1, grid),
        halo_rows.reshape(1, n * halo),
        edge_src_dev.reshape(1, edges),
        edge_src_slot.reshape(1, edges),
        edge_dst.reshape(1, edges),
    )


def solution(mesh):
    both = ("band", "dom")
    return jax.shard_map(
        functools.partial(body, bands=mesh.shape["band"], doms=mesh.shape["dom"]),
        mesh=mesh,
        in_specs=(P(both, None),) * 4
        + (P(),) * 7
        + (P(both, None), P(both), P(both, None, None), P(both), P(both), P(both)),
        out_specs=(P(both, None), P("band", "dom")),
        check_vma=False,
    )
```

```python
import functools

import jax
import jax.numpy as jnp
from jax import lax
from jax.experimental import pallas as pl
from jax.experimental.pallas import tpu as pltpu
from jax.sharding import PartitionSpec as P

MESH = pl.DeviceIdType.MESH
F32 = jnp.float32
BF16 = jnp.bfloat16
CHUNKS = 8
EARLY = 2
INPUTS = 17
STRIDE = 53
STRIDE_INVERSE = 29


def sigmoid(value):
    return 0.5 * jnp.tanh(0.5 * value) + 0.5


def dot(a, b):
    return jnp.dot(a, b, preferred_element_type=F32)


def dot_t(a, b):
    return lax.dot_general(a, b, (((1,), (1,)), ((), ())), preferred_element_type=F32)


def one_hot(mask):
    return jnp.where(mask, 1.0, 0.0).astype(BF16)


def iota(shape, dim):
    return lax.broadcasted_iota(jnp.int32, shape, dim)


def column(row):
    wide = jnp.broadcast_to(row.astype(F32), (8, row.shape[1]))
    return jnp.transpose(wide)[:, :1].astype(jnp.int32)


def moments(values):
    center = values - jnp.mean(values, axis=-1, keepdims=True)
    spread = jnp.mean(center * center, axis=-1, keepdims=True)
    scale = lax.rsqrt(spread + 1e-05)
    return center * scale, scale


def fold(values, parts, depth):
    half = values.shape[1] // 2
    cut = values.reshape(parts, depth, 2 * half)
    return jnp.concatenate([cut[:, :, :half], cut[:, :, half:]], axis=1).astype(BF16)


def unfold(values):
    parts, twice, half = values.shape
    depth = twice // 2
    wide = values.astype(F32)
    return jnp.concatenate([wide[:, :depth], wide[:, depth:]], axis=2).reshape(parts * depth, 2 * half)


def kernel(
    nx,
    nz,
    ny,
    cap,
    halo,
    *refs,
):
    inputs, refs = refs[:INPUTS], refs[INPUTS:]
    pred_ref, grad_ref, *refs = refs
    held, loaded, refs = refs[:INPUTS], refs[INPUTS], refs[INPUTS + 1 :]
    (
        x_ref,
        ml_ref,
        es_ref,
        cot_ref,
        wemb_ref,
        wsend_ref,
        wrecv_ref,
        wedge_ref,
        wm_ref,
        wg_ref,
        wp_ref,
        owner_ref,
        local_ref,
        halo_ref,
        dev_ref,
        slot_ref,
        dst_ref,
    ) = held
    (
        xs,
        cs,
        web,
        wpp,
        wpt,
        slots,
        sbuf,
        rbuf,
        csbuf,
        crbuf,
        obuf,
        inbuf,
        bsend,
        bland,
        hbuf,
        own,
        ownt,
        query,
        agg,
        enc,
        hal,
        osnd,
        orcv,
        orcvt,
        part,
        est,
        inb,
        snd,
        esum,
        mesh_part,
        dz,
        dsum,
        dpre,
        gland,
        g2,
        gl2,
        pick,
        a_send,
        a_recv,
        c_send,
        c_recv,
        h_send,
        h_recv,
        b_send,
        b_recv,
        p_send,
        p_recv,
        g_send,
        g_recv,
    ) = refs
    n = nx * nz * 2 * ny
    chips = nx * nz * ny
    width_in, grid = x_ref.shape
    nodes, width = ml_ref.shape
    edges = es_ref.shape[0]
    outs = cot_ref.shape[0]
    spc = n // CHUNKS
    rows = spc * cap
    epc = edges // CHUNKS
    band, y = lax.axis_index("band"), lax.axis_index("dom")
    k = lax.rem(band, 2)
    me = band * ny + y

    def shift(r, sign):
        to = lax.rem(me + r * (STRIDE if sign > 0 else n - STRIDE % n), n)
        return lax.div(to, ny), lax.rem(to, ny)

    barrier = pltpu.get_barrier_semaphore()

    def greet(r, carry):
        pl.semaphore_signal(barrier, inc=1, device_id=shift(r, 1), device_id_type=MESH)
        return carry

    lax.fori_loop(1, n, greet, 0)

    order = (11, 12, 0, 3, 1, 4, 6, 16, 14, 15, 2, 7, 13, 10, 5, 9, 8)
    for i in order:
        pltpu.make_async_copy(inputs[i], held[i], loaded.at[i]).start()

    def ready(*which):
        for i in which:
            pltpu.make_async_copy(inputs[i], held[i], loaded.at[i]).wait()

    ready(11, 12)
    o = owner_ref[...]
    member = jnp.where(o == iota((n, grid), 0), 1.0, 0.0)
    tri = min(128, grid)
    before = one_hot(iota((tri, tri), 0) < iota((tri, tri), 1))
    base = jnp.zeros((n, 1), F32)
    ranks = []
    for i in range(grid // tri):
        m = member[:, i * tri : (i + 1) * tri]
        count = dot(m.astype(BF16), before) + base
        ranks.append(jnp.sum(count * m, axis=0, keepdims=True))
        base = base + jnp.sum(m, axis=1, keepdims=True)
    rank = jnp.concatenate(ranks, axis=1).astype(jnp.int32)
    slots[...] = (((o - me) * STRIDE_INVERSE) & (n - 1)) * cap + rank

    ready(0, 3)
    first = width_in // 16 * 16
    xs[first:, :] = jnp.zeros((width - first, grid), BF16)
    xs[:width_in, :] = x_ref[...]
    tail = xs[first : first + 16, :].astype(F32)
    mark = iota((16, grid), 0) == width_in - first
    xs[first : first + 16, :] = jnp.where(mark, (local_ref[...] + 1).astype(F32), tail).astype(BF16)
    first = outs // 16 * 16
    cs[first:, :] = jnp.zeros((cs.shape[0] - first, grid), BF16)
    cs[:outs, :] = cot_ref[...]

    pl.semaphore_wait(barrier, n - 1)

    def send(src, dst, send_sem, recv_sem, to):
        pltpu.make_async_remote_copy(
            src_ref=src, dst_ref=dst, send_sem=send_sem, recv_sem=recv_sem, device_id=to, device_id_type=MESH
        ).start()

    def take(ref, sem):
        pltpu.make_async_copy(ref, ref, sem).wait()

    def send_parts(c, src, dst, send_sem, recv_sem, sign):
        def one(i, carry):
            r = c * spc + i

            @pl.when(r > 0)
            def _():
                send(src.at[r], dst.at[r], send_sem, recv_sem.at[c], shift(r, sign))

            return carry

        lax.fori_loop(0, spc, one, 0)

        @pl.when(c == 0)
        def _():
            pltpu.make_async_copy(src.at[0], dst.at[0], recv_sem.at[0]).start()

    def pack(c, carry):
        place = one_hot(slots[...] == iota((rows, grid), 0) + c * rows)
        pick[pl.ds(pl.multiple_of(c * rows, rows), rows), :] = place
        sbuf[pl.ds(c * spc, spc)] = fold(dot_t(place, xs[...]), spc, cap)
        send_parts(c, sbuf, rbuf, a_send, a_recv, 1)
        csbuf[pl.ds(c * spc, spc)] = fold(dot_t(place, cs[...]), spc, cap)
        return carry

    lax.fori_loop(0, CHUNKS, pack, 0)

    def send_cot(c, carry):
        send_parts(c, csbuf, crbuf, c_send, c_recv, 1)
        return carry

    ready(1, 4, 6, 16, 14, 15, 2, 7, 13, 10, 5, 9, 8)
    first = width_in // 16 * 16
    web[first:, :] = jnp.zeros((width - first, width), BF16)
    web[:width_in, :] = wemb_ref[...]
    first = outs // 16 * 16
    wpt[first:, :] = jnp.zeros((wpt.shape[0] - first, width), BF16)
    wpt[:outs, :] = wp_ref[...]
    wpp[...] = jnp.transpose(wpt[...])
    halo_col = jnp.transpose(halo_ref[...].astype(F32)).astype(BF16)
    query[...] = dot(ml_ref[...], wrecv_ref[...]).astype(BF16)

    def encode(c, carry):
        take(rbuf.at[pl.ds(c * spc, spc)], a_recv.at[c])

        @pl.when(c == CHUNKS - 1)
        def _():
            lax.fori_loop(0, EARLY, send_cot, 0)

        wide = unfold(rbuf[pl.ds(c * spc, spc)])
        mark = iota((rows, 128), 1) == width_in - (width - 128)
        label = jnp.sum(jnp.where(mark, wide[:, width - 128 :], 0.0), axis=1, keepdims=True)
        hit = one_hot(label.astype(jnp.int32) - 1 == iota((rows, nodes), 1))
        lines = pl.ds(pl.multiple_of(c * rows, rows), rows)
        own[lines, :] = hit
        hit_t = jnp.transpose(hit)
        ownt[:, lines] = hit_t
        hid = dot(wide.astype(BF16), web[...])
        hid = (hid * sigmoid(hid)).astype(BF16)
        hbuf[lines, :] = hid
        arg = dot(hid, wsend_ref[...]) + dot(hit, query[...])
        agg[...] += dot(hit_t, (arg * sigmoid(arg)).astype(BF16))
        return carry

    def prepare(c, carry):
        lines = pl.ds(pl.multiple_of(c * epc, epc), epc)
        dst = dst_ref[:, lines]
        orcvt[:, lines] = one_hot(dst == iota((nodes, epc), 0))
        orcv[lines, :] = one_hot(column(dst) == iota((epc, nodes), 1))
        source = column(dev_ref[:, lines] * halo + slot_ref[:, lines])
        osnd[lines, :] = one_hot(source == iota((epc, n * halo), 1))
        state = es_ref[lines, :]
        est[:, lines] = jnp.transpose(state)
        part[lines, :] = dot(state, wedge_ref[:width, :])
        hpc = n * halo // CHUNKS
        spots = pl.ds(pl.multiple_of(c * hpc, hpc), hpc)
        to = (me + (iota((hpc, n), 0) + c * hpc) // halo * STRIDE) & (n - 1)
        spread = one_hot(to == iota((hpc, n), 1))
        label = jnp.where(iota((hpc, halo), 0) % halo == iota((hpc, halo), 1), dot(spread, halo_col), 0.0)
        label = jnp.sum(label, axis=1, keepdims=True).astype(jnp.int32)
        hal[spots, :] = one_hot(label == iota((hpc, nodes), 1))
        return carry

    lax.fori_loop(0, CHUNKS, prepare, 0)
    agg[...] = jnp.zeros_like(agg)
    lax.fori_loop(0, CHUNKS, encode, 0)

    encoded = (ml_ref[...].astype(F32) + moments(agg[...])[0]).astype(BF16)
    enc[...] = encoded

    def outbound(c, carry):
        hpc = n * halo // CHUNKS
        spots = pl.ds(pl.multiple_of(c * hpc, hpc), hpc)
        obuf[pl.ds(c * spc, spc)] = fold(dot(hal[spots, :], enc[...]), spc, halo)

        def one(i, inner):
            r = c * spc + i

            @pl.when(r > 0)
            def _():
                send(obuf.at[r], inbuf.at[me], h_send, h_recv, shift(r, 1))

            return inner

        lax.fori_loop(0, spc, one, 0)
        return carry

    lax.fori_loop(0, CHUNKS, outbound, 0)
    pltpu.make_async_copy(obuf.at[0], inbuf.at[me], h_recv).start()
    lax.fori_loop(EARLY, CHUNKS, send_cot, 0)

    own_part = dot(enc[...], wedge_ref[2 * width :, :]).astype(BF16)
    mesh_part[...] = own_part

    def edge_own(c, carry):
        lines = pl.ds(pl.multiple_of(c * epc, epc), epc)
        part[lines, :] += dot(orcv[lines, :], mesh_part[...])
        return carry

    lax.fori_loop(0, CHUNKS, edge_own, 0)
    esum[...] = jnp.zeros_like(esum)
    take(inbuf, h_recv)
    inb[...] = unfold(inbuf[...]).astype(BF16)

    def edge_forward(c, carry):
        lines = pl.ds(pl.multiple_of(c * epc, epc), epc)
        sender = dot(osnd[lines, :], inb[...]).astype(BF16)
        snd[lines, :] = sender
        pre = part[lines, :] + dot(sender, wedge_ref[width : 2 * width, :])
        part[lines, :] = pre
        esum[...] += dot(orcvt[:, lines], (pre * sigmoid(pre)).astype(BF16))
        return carry

    lax.fori_loop(0, CHUNKS, edge_forward, 0)
    normed, scale = moments(esum[...])
    updated = (enc[...].astype(F32) + normed).astype(BF16)
    mesh_part[...] = dot(updated, wm_ref[...]).astype(BF16)
    dz[...] = jnp.zeros_like(dz)

    def decode(c, carry):
        lines = pl.ds(pl.multiple_of(c * rows, rows), rows)
        zed = dot(hbuf[lines, :], wg_ref[...]) + dot(own[lines, :], mesh_part[...])
        sig = sigmoid(zed)
        bsend[pl.ds(c * spc, spc)] = fold(dot((zed * sig).astype(BF16), wpp[...]), spc, cap)

        def one(i, inner):
            r = c * spc + i

            @pl.when(r > 0)
            def _():
                send(bsend.at[r], bland.at[r], b_send, b_recv, shift(r, -1))

            return inner

        lax.fori_loop(0, spc, one, 0)
        take(crbuf.at[pl.ds(c * spc, spc)], c_recv.at[c])
        slope = dot(unfold(crbuf[pl.ds(c * spc, spc)]).astype(BF16), wpt[...])
        slope = (slope * sig * (1.0 + zed * (1.0 - sig))).astype(BF16)
        dz[...] += dot(ownt[:, lines], slope)
        return carry

    lax.fori_loop(0, CHUNKS, decode, 0)
    pltpu.make_async_copy(bsend.at[0], bland.at[0], b_recv).start()

    slope = lax.dot_general(
        dz[...].astype(BF16), wm_ref[...], (((1,), (1,)), ((), ())), preferred_element_type=F32
    )
    normed, scale = moments(esum[...])
    slope = scale * (
        slope
        - jnp.mean(slope, axis=-1, keepdims=True)
        - normed * jnp.mean(slope * normed, axis=-1, keepdims=True)
    )
    dsum[...] = slope.astype(BF16)

    def edge_backward(c, carry):
        lines = pl.ds(pl.multiple_of(c * epc, epc), epc)
        pre = part[lines, :]
        sig = sigmoid(pre)
        slope = dot(orcv[lines, :], dsum[...])
        dpre[lines, :] = (slope * sig * (1.0 + pre * (1.0 - sig))).astype(BF16)
        return carry

    lax.fori_loop(0, CHUNKS, edge_backward, 0)
    share = 3 * width // (nx * nz * 2)

    def send_pair(i, carry):
        block = pl.ds(pl.multiple_of((i * 2 + 1 - k) * share, 16), share)
        send(hbuf.at[block, :], gland.at[i], p_send, p_recv, (band + 1 - 2 * k, y))
        return carry

    hbuf[:width, :] = dot(est[...], dpre[...]).astype(BF16)
    cut = width // (2 * share)
    lax.fori_loop(0, cut, send_pair, 0)
    hbuf[width : 2 * width, :] = lax.dot_general(
        snd[...], dpre[...], (((0,), (0,)), ((), ())), preferred_element_type=F32
    ).astype(BF16)
    cut, done = 2 * width // (2 * share), cut
    lax.fori_loop(done, cut, send_pair, 0)
    received = dot(orcvt[...], dpre[...]).astype(BF16)
    hbuf[2 * width : 3 * width, :] = lax.dot_general(
        enc[...], received, (((0,), (0,)), ((), ())), preferred_element_type=F32
    ).astype(BF16)
    lax.fori_loop(cut, nx * nz, send_pair, 0)
    take(gland, p_recv)
    cols = width // ny

    def add_pair(i, carry):
        block = pl.ds(pl.multiple_of((i * 2 + k) * share, 16), share)
        both = (hbuf[block, :].astype(F32) + gland[i].astype(F32)).astype(BF16)
        for d in range(ny):
            g2[i * ny + d] = both[:, d * cols : (d + 1) * cols]
        return carry

    lax.fori_loop(0, nx * nz, add_pair, 0)
    chip = lax.div(band, 2) * ny + y

    def send_grad(r, carry):
        to = lax.rem(chip + r * STRIDE, chips)
        xz = lax.div(to, ny)
        send(g2.at[to], gl2.at[chip], g_send, g_recv, (xz * 2 + k, lax.rem(to, ny)))
        return carry

    lax.fori_loop(1, chips, send_grad, 0)
    pltpu.make_async_copy(g2.at[chip], gl2.at[chip], g_recv).start()

    take(bland, b_recv)

    def arrange(c, carry):
        lines = pl.ds(pl.multiple_of(c * rows, rows), rows)
        ownt[:, lines] = jnp.transpose(unfold(bland[pl.ds(c * spc, spc)]).astype(BF16))
        return carry

    lax.fori_loop(0, CHUNKS, arrange, 0)
    gpc = min(256, grid)

    def choose(c, carry):
        spots = pl.ds(pl.multiple_of(c * gpc, gpc), gpc)
        pred_ref[:, spots] = dot(ownt[...], pick[:, spots])[:outs].astype(BF16)
        return carry

    lax.fori_loop(0, grid // gpc, choose, 0)
    take(gl2, g_recv)
    grad_ref[...] = jnp.zeros_like(grad_ref)

    def add_grad(i, carry):
        grad_ref[...] += gl2[i].astype(F32)
        return carry

    lax.fori_loop(0, chips, add_grad, 0)
    take(sbuf.at[pl.ds(1, n - 1)], a_send)
    take(csbuf.at[pl.ds(1, n - 1)], c_send)
    take(obuf.at[pl.ds(1, n - 1)], h_send)
    take(bsend.at[pl.ds(1, n - 1)], b_send)
    take(gland, p_send)
    take(g2.at[pl.ds(1, chips - 1)], g_send)


def body(
    grid_inputs,
    mesh_latent,
    edge_state,
    cotangent,
    w_embed,
    w_send,
    w_recv,
    w_edge,
    w_mesh_out,
    w_grid_out,
    w_predict,
    enc_owner,
    enc_local,
    halo_rows,
    edge_src_dev,
    edge_src_slot,
    edge_dst,
    bands,
    doms,
):
    side = int(round((bands // 2) ** 0.5))
    n = bands * doms
    chips = n // 2
    grid = grid_inputs.shape[0]
    nodes, width = mesh_latent.shape
    edges = edge_state.shape[0]
    outs = cotangent.shape[1]
    wide_out = 256
    cap = 3 * grid // n
    halo = halo_rows.shape[2]
    share, cols = 3 * width // bands, width // doms
    vmem = pltpu.VMEM
    scratch = [
        vmem((width, grid), BF16),
        vmem((wide_out, grid), BF16),
        vmem((width, width), BF16),
        vmem((width, wide_out), BF16),
        vmem((wide_out, width), BF16),
        vmem((1, grid), jnp.int32),
        vmem((n, 2 * cap, width // 2), BF16),
        vmem((n, 2 * cap, width // 2), BF16),
        vmem((n, 2 * cap, wide_out // 2), BF16),
        vmem((n, 2 * cap, wide_out // 2), BF16),
        vmem((n, 2 * halo, width // 2), BF16),
        vmem((n, 2 * halo, width // 2), BF16),
        vmem((n, 2 * cap, wide_out // 2), BF16),
        vmem((n, 2 * cap, wide_out // 2), BF16),
        vmem((max(n * cap, 3 * width), width), BF16),
        vmem((n * cap, nodes), BF16),
        vmem((nodes, n * cap), BF16),
        vmem((nodes, width), BF16),
        vmem((nodes, width), F32),
        vmem((nodes, width), BF16),
        vmem((n * halo, nodes), BF16),
        vmem((edges, n * halo), BF16),
        vmem((edges, nodes), BF16),
        vmem((nodes, edges), BF16),
        vmem((edges, width), F32),
        vmem((width, edges), BF16),
        vmem((n * halo, width), BF16),
        vmem((edges, width), BF16),
        vmem((nodes, width), F32),
        vmem((nodes, width), BF16),
        vmem((nodes, width), F32),
        vmem((nodes, width), BF16),
        vmem((edges, width), BF16),
        vmem((bands // 2, share, width), BF16),
        vmem((chips, share, cols), BF16),
        vmem((chips, share, cols), BF16),
        vmem((n * cap, grid), BF16),
    ]
    dma = pltpu.SemaphoreType.DMA
    for _ in range(2):
        scratch += [dma, dma((CHUNKS,))]
    scratch += [dma] * 8
    operands = (
        grid_inputs.T,
        mesh_latent,
        edge_state,
        cotangent.T,
        w_embed,
        w_send,
        w_recv,
        w_edge,
        w_mesh_out,
        w_grid_out,
        w_predict.T,
        enc_owner.reshape(1, grid),
        enc_local.reshape(1, grid),
        halo_rows[0].T,
        edge_src_dev.reshape(1, edges),
        edge_src_slot.reshape(1, edges),
        edge_dst.reshape(1, edges),
    )
    scratch = [vmem(a.shape, a.dtype) for a in operands] + [pltpu.SemaphoreType.DMA((INPUTS,))] + scratch
    prediction, gradient = pl.pallas_call(
        functools.partial(kernel, side, side, doms, cap, halo),
        out_shape=(
            jax.ShapeDtypeStruct((outs, grid), BF16),
            jax.ShapeDtypeStruct((share, cols), F32),
        ),
        in_specs=[pl.BlockSpec(memory_space=pl.ANY)] * INPUTS,
        out_specs=(pl.BlockSpec(memory_space=vmem),) * 2,
        scratch_shapes=scratch,
        compiler_params=pltpu.CompilerParams(
            collective_id=0, has_side_effects=True, vmem_limit_bytes=63 * 1024 * 1024
        ),
        cost_estimate=pl.CostEstimate(flops=25 * 10**9, bytes_accessed=10**7, transcendentals=10**7),
    )(*operands)
    return prediction.T, gradient


def solution(mesh):
    both = ("band", "dom")
    return jax.shard_map(
        functools.partial(body, bands=mesh.shape["band"], doms=mesh.shape["dom"]),
        mesh=mesh,
        in_specs=(P(both, None),) * 4
        + (P(),) * 7
        + (P(both, None), P(both), P(both, None, None), P(both), P(both), P(both)),
        out_specs=(P(both, None), P("band", "dom")),
        check_vma=False,
    )
```

```python
import functools

import jax
import jax.numpy as jnp
from jax import lax
from jax.experimental import pallas as pl
from jax.experimental.pallas import tpu as pltpu
from jax.sharding import PartitionSpec as P

MESH = pl.DeviceIdType.MESH
F32 = jnp.float32
BF16 = jnp.bfloat16
CHUNKS = 8
INPUTS = 17
STRIDE = 53
STRIDE_INVERSE = 29


def sigmoid(value):
    return 0.5 * jnp.tanh(0.5 * value) + 0.5


def dot(a, b):
    return jnp.dot(a, b, preferred_element_type=F32)


def dot_t(a, b):
    return lax.dot_general(a, b, (((1,), (1,)), ((), ())), preferred_element_type=F32)


def one_hot(mask):
    return jnp.where(mask, 1.0, 0.0).astype(BF16)


def iota(shape, dim):
    return lax.broadcasted_iota(jnp.int32, shape, dim)


def column(row):
    wide = jnp.broadcast_to(row.astype(F32), (8, row.shape[1]))
    return jnp.transpose(wide)[:, :1].astype(jnp.int32)


def moments(values):
    center = values - jnp.mean(values, axis=-1, keepdims=True)
    spread = jnp.mean(center * center, axis=-1, keepdims=True)
    scale = lax.rsqrt(spread + 1e-05)
    return center * scale, scale


def fold(values, parts, depth):
    half = values.shape[1] // 2
    cut = values.reshape(parts, depth, 2 * half)
    return jnp.concatenate([cut[:, :, :half], cut[:, :, half:]], axis=1).astype(BF16)


def unfold(values):
    parts, twice, half = values.shape
    depth = twice // 2
    wide = values.astype(F32)
    return jnp.concatenate([wide[:, :depth], wide[:, depth:]], axis=2).reshape(parts * depth, 2 * half)


def kernel(
    nx,
    nz,
    ny,
    cap,
    halo,
    *refs,
):
    inputs, refs = refs[:INPUTS], refs[INPUTS:]
    pred_ref, grad_ref, *refs = refs
    held, loaded, refs = refs[:INPUTS], refs[INPUTS], refs[INPUTS + 1 :]
    (
        x_ref,
        ml_ref,
        es_ref,
        cot_ref,
        wemb_ref,
        wsend_ref,
        wrecv_ref,
        wedge_ref,
        wm_ref,
        wg_ref,
        wp_ref,
        owner_ref,
        local_ref,
        halo_ref,
        dev_ref,
        slot_ref,
        dst_ref,
    ) = held
    (
        xs,
        cs,
        web,
        wpp,
        wpt,
        slots,
        sbuf,
        rbuf,
        csbuf,
        crbuf,
        obuf,
        inbuf,
        bsend,
        bland,
        hbuf,
        own,
        ownt,
        query,
        agg,
        enc,
        hal,
        osnd,
        orcv,
        orcvt,
        part,
        est,
        inb,
        snd,
        esum,
        mesh_part,
        dz,
        dsum,
        dpre,
        gland,
        line1,
        land1,
        line2,
        land2,
        pick,
        a_send,
        a_recv,
        c_send,
        c_recv,
        h_send,
        h_recv,
        b_send,
        b_recv,
        p_send,
        p_recv,
        q_send,
        q_recv,
        g_send,
        g_recv,
    ) = refs
    n = nx * nz * 2 * ny
    width_in, grid = x_ref.shape
    nodes, width = ml_ref.shape
    edges = es_ref.shape[0]
    outs = cot_ref.shape[0]
    spc = n // CHUNKS
    rows = spc * cap
    epc = edges // CHUNKS
    band, y = lax.axis_index("band"), lax.axis_index("dom")
    k = lax.rem(band, 2)
    me = band * ny + y

    def shift(r, sign):
        to = lax.rem(me + r * (STRIDE if sign > 0 else n - STRIDE % n), n)
        return lax.div(to, ny), lax.rem(to, ny)

    barrier = pltpu.get_barrier_semaphore()

    def greet(r, carry):
        pl.semaphore_signal(barrier, inc=1, device_id=shift(r, 1), device_id_type=MESH)
        return carry

    lax.fori_loop(1, n, greet, 0)

    order = (11, 12, 0, 3, 1, 4, 6, 16, 14, 15, 2, 7, 13, 10, 5, 9, 8)
    for i in order:
        pltpu.make_async_copy(inputs[i], held[i], loaded.at[i]).start()

    def ready(*which):
        for i in which:
            pltpu.make_async_copy(inputs[i], held[i], loaded.at[i]).wait()

    ready(11, 12)
    o = owner_ref[...]
    member = jnp.where(o == iota((n, grid), 0), 1.0, 0.0)
    tri = min(128, grid)
    before = one_hot(iota((tri, tri), 0) < iota((tri, tri), 1))
    base = jnp.zeros((n, 1), F32)
    ranks = []
    for i in range(grid // tri):
        m = member[:, i * tri : (i + 1) * tri]
        count = dot(m.astype(BF16), before) + base
        ranks.append(jnp.sum(count * m, axis=0, keepdims=True))
        base = base + jnp.sum(m, axis=1, keepdims=True)
    rank = jnp.concatenate(ranks, axis=1).astype(jnp.int32)
    slots[...] = (((o - me) * STRIDE_INVERSE) & (n - 1)) * cap + rank

    ready(0, 3)
    first = width_in // 16 * 16
    xs[first:, :] = jnp.zeros((width - first, grid), BF16)
    xs[:width_in, :] = x_ref[...]
    tail = xs[first : first + 16, :].astype(F32)
    mark = iota((16, grid), 0) == width_in - first
    xs[first : first + 16, :] = jnp.where(mark, (local_ref[...] + 1).astype(F32), tail).astype(BF16)
    first = outs // 16 * 16
    cs[first:, :] = jnp.zeros((cs.shape[0] - first, grid), BF16)
    cs[:outs, :] = cot_ref[...]

    pl.semaphore_wait(barrier, n - 1)

    def send(src, dst, send_sem, recv_sem, to):
        pltpu.make_async_remote_copy(
            src_ref=src, dst_ref=dst, send_sem=send_sem, recv_sem=recv_sem, device_id=to, device_id_type=MESH
        ).start()

    def take(ref, sem):
        pltpu.make_async_copy(ref, ref, sem).wait()

    def send_parts(c, src, dst, send_sem, recv_sem, sign):
        def one(i, carry):
            r = c * spc + i

            @pl.when(r > 0)
            def _():
                send(src.at[r], dst.at[r], send_sem, recv_sem.at[c], shift(r, sign))

            return carry

        lax.fori_loop(0, spc, one, 0)

        @pl.when(c == 0)
        def _():
            pltpu.make_async_copy(src.at[0], dst.at[0], recv_sem.at[0]).start()

    def pack(c, carry):
        place = one_hot(slots[...] == iota((rows, grid), 0) + c * rows)
        pick[pl.ds(pl.multiple_of(c * rows, rows), rows), :] = place
        sbuf[pl.ds(c * spc, spc)] = fold(dot_t(place, xs[...]), spc, cap)
        send_parts(c, sbuf, rbuf, a_send, a_recv, 1)
        csbuf[pl.ds(c * spc, spc)] = fold(dot_t(place, cs[...]), spc, cap)
        return carry

    lax.fori_loop(0, CHUNKS, pack, 0)

    def send_cot(c, carry):
        send_parts(c, csbuf, crbuf, c_send, c_recv, 1)
        return carry

    ready(1, 4, 6, 16, 14, 15, 2, 7, 13, 10, 5, 9, 8)
    first = width_in // 16 * 16
    web[first:, :] = jnp.zeros((width - first, width), BF16)
    web[:width_in, :] = wemb_ref[...]
    first = outs // 16 * 16
    wpt[first:, :] = jnp.zeros((wpt.shape[0] - first, width), BF16)
    wpt[:outs, :] = wp_ref[...]
    wpp[...] = jnp.transpose(wpt[...])
    halo_col = jnp.transpose(halo_ref[...].astype(F32)).astype(BF16)
    query[...] = dot(ml_ref[...], wrecv_ref[...]).astype(BF16)

    def encode(c, carry):
        take(rbuf.at[pl.ds(c * spc, spc)], a_recv.at[c])
        wide = unfold(rbuf[pl.ds(c * spc, spc)])
        mark = iota((rows, 128), 1) == width_in - (width - 128)
        label = jnp.sum(jnp.where(mark, wide[:, width - 128 :], 0.0), axis=1, keepdims=True)
        hit = one_hot(label.astype(jnp.int32) - 1 == iota((rows, nodes), 1))
        lines = pl.ds(pl.multiple_of(c * rows, rows), rows)
        own[lines, :] = hit
        hit_t = jnp.transpose(hit)
        ownt[:, lines] = hit_t
        hid = dot(wide.astype(BF16), web[...])
        hid = (hid * sigmoid(hid)).astype(BF16)
        hbuf[lines, :] = hid
        arg = dot(hid, wsend_ref[...]) + dot(hit, query[...])
        agg[...] += dot(hit_t, (arg * sigmoid(arg)).astype(BF16))
        return carry

    def prepare(c, carry):
        lines = pl.ds(pl.multiple_of(c * epc, epc), epc)
        dst = dst_ref[:, lines]
        orcvt[:, lines] = one_hot(dst == iota((nodes, epc), 0))
        orcv[lines, :] = one_hot(column(dst) == iota((epc, nodes), 1))
        source = column(dev_ref[:, lines] * halo + slot_ref[:, lines])
        osnd[lines, :] = one_hot(source == iota((epc, n * halo), 1))
        state = es_ref[lines, :]
        est[:, lines] = jnp.transpose(state)
        part[lines, :] = dot(state, wedge_ref[:width, :])
        hpc = n * halo // CHUNKS
        spots = pl.ds(pl.multiple_of(c * hpc, hpc), hpc)
        to = (me + (iota((hpc, n), 0) + c * hpc) // halo * STRIDE) & (n - 1)
        spread = one_hot(to == iota((hpc, n), 1))
        label = jnp.where(iota((hpc, halo), 0) % halo == iota((hpc, halo), 1), dot(spread, halo_col), 0.0)
        label = jnp.sum(label, axis=1, keepdims=True).astype(jnp.int32)
        hal[spots, :] = one_hot(label == iota((hpc, nodes), 1))
        return carry

    lax.fori_loop(0, CHUNKS, prepare, 0)
    agg[...] = jnp.zeros_like(agg)
    lax.fori_loop(0, CHUNKS, encode, 0)

    encoded = (ml_ref[...].astype(F32) + moments(agg[...])[0]).astype(BF16)
    enc[...] = encoded

    def outbound(c, carry):
        hpc = n * halo // CHUNKS
        spots = pl.ds(pl.multiple_of(c * hpc, hpc), hpc)
        obuf[pl.ds(c * spc, spc)] = fold(dot(hal[spots, :], enc[...]), spc, halo)

        def one(i, inner):
            r = c * spc + i

            @pl.when(r > 0)
            def _():
                send(obuf.at[r], inbuf.at[me], h_send, h_recv, shift(r, 1))

            return inner

        lax.fori_loop(0, spc, one, 0)
        return carry

    lax.fori_loop(0, CHUNKS, outbound, 0)
    pltpu.make_async_copy(obuf.at[0], inbuf.at[me], h_recv).start()
    lax.fori_loop(0, CHUNKS, send_cot, 0)

    own_part = dot(enc[...], wedge_ref[2 * width :, :]).astype(BF16)
    mesh_part[...] = own_part

    def edge_own(c, carry):
        lines = pl.ds(pl.multiple_of(c * epc, epc), epc)
        part[lines, :] += dot(orcv[lines, :], mesh_part[...])
        return carry

    lax.fori_loop(0, CHUNKS, edge_own, 0)
    esum[...] = jnp.zeros_like(esum)
    take(inbuf, h_recv)
    inb[...] = unfold(inbuf[...]).astype(BF16)

    def edge_forward(c, carry):
        lines = pl.ds(pl.multiple_of(c * epc, epc), epc)
        sender = dot(osnd[lines, :], inb[...]).astype(BF16)
        snd[lines, :] = sender
        pre = part[lines, :] + dot(sender, wedge_ref[width : 2 * width, :])
        part[lines, :] = pre
        esum[...] += dot(orcvt[:, lines], (pre * sigmoid(pre)).astype(BF16))
        return carry

    lax.fori_loop(0, CHUNKS, edge_forward, 0)
    normed, scale = moments(esum[...])
    updated = (enc[...].astype(F32) + normed).astype(BF16)
    mesh_part[...] = dot(updated, wm_ref[...]).astype(BF16)
    dz[...] = jnp.zeros_like(dz)

    def decode(c, carry):
        lines = pl.ds(pl.multiple_of(c * rows, rows), rows)
        zed = dot(hbuf[lines, :], wg_ref[...]) + dot(own[lines, :], mesh_part[...])
        sig = sigmoid(zed)
        bsend[pl.ds(c * spc, spc)] = fold(dot((zed * sig).astype(BF16), wpp[...]), spc, cap)

        def one(i, inner):
            r = c * spc + i

            @pl.when(r > 0)
            def _():
                send(bsend.at[r], bland.at[r], b_send, b_recv, shift(r, -1))

            return inner

        lax.fori_loop(0, spc, one, 0)
        take(crbuf.at[pl.ds(c * spc, spc)], c_recv.at[c])
        slope = dot(unfold(crbuf[pl.ds(c * spc, spc)]).astype(BF16), wpt[...])
        slope = (slope * sig * (1.0 + zed * (1.0 - sig))).astype(BF16)
        dz[...] += dot(ownt[:, lines], slope)
        return carry

    lax.fori_loop(0, CHUNKS, decode, 0)
    pltpu.make_async_copy(bsend.at[0], bland.at[0], b_recv).start()

    slope = lax.dot_general(
        dz[...].astype(BF16), wm_ref[...], (((1,), (1,)), ((), ())), preferred_element_type=F32
    )
    normed, scale = moments(esum[...])
    slope = scale * (
        slope
        - jnp.mean(slope, axis=-1, keepdims=True)
        - normed * jnp.mean(slope * normed, axis=-1, keepdims=True)
    )
    dsum[...] = slope.astype(BF16)

    def edge_backward(c, carry):
        lines = pl.ds(pl.multiple_of(c * epc, epc), epc)
        pre = part[lines, :]
        sig = sigmoid(pre)
        slope = dot(orcv[lines, :], dsum[...])
        dpre[lines, :] = (slope * sig * (1.0 + pre * (1.0 - sig))).astype(BF16)
        return carry

    lax.fori_loop(0, CHUNKS, edge_backward, 0)
    share = 3 * width // (nx * nz * 2)

    def send_pair(i, carry):
        block = pl.ds(pl.multiple_of((i * 2 + 1 - k) * share, 16), share)
        send(hbuf.at[block, :], gland.at[i], p_send, p_recv, (band + 1 - 2 * k, y))
        return carry

    hbuf[:width, :] = dot(est[...], dpre[...]).astype(BF16)
    cut = width // (2 * share)
    lax.fori_loop(0, cut, send_pair, 0)
    hbuf[width : 2 * width, :] = lax.dot_general(
        snd[...], dpre[...], (((0,), (0,)), ((), ())), preferred_element_type=F32
    ).astype(BF16)
    cut, done = 2 * width // (2 * share), cut
    lax.fori_loop(done, cut, send_pair, 0)
    received = dot(orcvt[...], dpre[...]).astype(BF16)
    hbuf[2 * width : 3 * width, :] = lax.dot_general(
        enc[...], received, (((0,), (0,)), ((), ())), preferred_element_type=F32
    ).astype(BF16)
    lax.fori_loop(cut, nx * nz, send_pair, 0)
    take(gland, p_recv)
    cols = width // ny
    third = share // 3
    place3 = (lax.div(band, 2 * nz), lax.rem(lax.div(band, 2), nz), y)

    def add_pair(i, carry):
        block = pl.ds(pl.multiple_of((i * 2 + k) * share, 16), share)
        both = (hbuf[block, :].astype(F32) + gland[i].astype(F32)).astype(BF16)
        tx, tz = lax.div(i, nz), lax.rem(i, nz)
        for d in range(ny):
            part3 = both[:, d * cols : (d + 1) * cols]
            line1[0, tx, tz * ny + d] = part3[:third]
            line1[1, tz, tx * ny + d] = part3[third : 2 * third]
            line1[2, d, i] = part3[2 * third :]
        return carry

    lax.fori_loop(0, nx * nz, add_pair, 0)

    def device(axis, along, rest):
        two = [lax.div(rest, ny), lax.rem(rest, ny)]
        tx, tz, ty = two[:axis] + [along] + two[axis:]
        return (tx * nz + tz) * 2 + k, ty

    def others(axis):
        a, b = place3[:axis] + place3[axis + 1 :]
        return a * ny + b

    for step in range(1, ny):
        for axis in range(3):
            to = lax.rem(place3[axis] + step, ny)
            send(
                line1.at[axis, to], land1.at[axis, step - 1], q_send, q_recv.at[axis], device(axis, to, others(axis))
            )
    for axis in range(3):
        take(land1.at[axis], q_recv.at[axis])
        total = line1[axis, place3[axis]].astype(F32)
        for step in range(1, ny):
            total += land1[axis, step - 1].astype(F32)
        line2[axis] = total.astype(BF16)
        mine = others(axis)

        def send_line(r, carry, axis=axis, mine=mine):
            to = lax.rem(mine + r * 5, ny * ny)
            send(line2.at[axis, to], land2.at[axis, mine], g_send, g_recv, device(axis, place3[axis], to))
            return carry

        lax.fori_loop(1, ny * ny, send_line, 0)
        pltpu.make_async_copy(line2.at[axis, mine], land2.at[axis, mine], g_recv).start()

    take(bland, b_recv)

    def arrange(c, carry):
        lines = pl.ds(pl.multiple_of(c * rows, rows), rows)
        ownt[:, lines] = jnp.transpose(unfold(bland[pl.ds(c * spc, spc)]).astype(BF16))
        return carry

    lax.fori_loop(0, CHUNKS, arrange, 0)
    gpc = min(256, grid)

    def choose(c, carry):
        spots = pl.ds(pl.multiple_of(c * gpc, gpc), gpc)
        pred_ref[:, spots] = dot(ownt[...], pick[:, spots])[:outs].astype(BF16)
        return carry

    lax.fori_loop(0, grid // gpc, choose, 0)
    take(land2, g_recv)
    for axis in range(3):
        grad_ref[axis * third : (axis + 1) * third, :] = jnp.sum(land2[axis].astype(F32), axis=0)
    take(sbuf.at[pl.ds(1, n - 1)], a_send)
    take(csbuf.at[pl.ds(1, n - 1)], c_send)
    take(obuf.at[pl.ds(1, n - 1)], h_send)
    take(bsend.at[pl.ds(1, n - 1)], b_send)
    take(gland, p_send)
    take(land1, q_send)
    take(land2.at[:, pl.ds(1, ny * ny - 1)], g_send)


def hand_over(pred_ref, grad_ref, pred_out, grad_out):
    pred_out[...] = pred_ref[...]
    grad_out[...] = grad_ref[...]


def body(
    grid_inputs,
    mesh_latent,
    edge_state,
    cotangent,
    w_embed,
    w_send,
    w_recv,
    w_edge,
    w_mesh_out,
    w_grid_out,
    w_predict,
    enc_owner,
    enc_local,
    halo_rows,
    edge_src_dev,
    edge_src_slot,
    edge_dst,
    bands,
    doms,
):
    side = int(round((bands // 2) ** 0.5))
    n = bands * doms
    grid = grid_inputs.shape[0]
    nodes, width = mesh_latent.shape
    edges = edge_state.shape[0]
    outs = cotangent.shape[1]
    wide_out = 256
    cap = 3 * grid // n
    halo = halo_rows.shape[2]
    share, cols = 3 * width // bands, width // doms
    vmem = pltpu.VMEM
    scratch = [
        vmem((width, grid), BF16),
        vmem((wide_out, grid), BF16),
        vmem((width, width), BF16),
        vmem((width, wide_out), BF16),
        vmem((wide_out, width), BF16),
        vmem((1, grid), jnp.int32),
        vmem((n, 2 * cap, width // 2), BF16),
        vmem((n, 2 * cap, width // 2), BF16),
        vmem((n, 2 * cap, wide_out // 2), BF16),
        vmem((n, 2 * cap, wide_out // 2), BF16),
        vmem((n, 2 * halo, width // 2), BF16),
        vmem((n, 2 * halo, width // 2), BF16),
        vmem((n, 2 * cap, wide_out // 2), BF16),
        vmem((n, 2 * cap, wide_out // 2), BF16),
        vmem((max(n * cap, 3 * width), width), BF16),
        vmem((n * cap, nodes), BF16),
        vmem((nodes, n * cap), BF16),
        vmem((nodes, width), BF16),
        vmem((nodes, width), F32),
        vmem((nodes, width), BF16),
        vmem((n * halo, nodes), BF16),
        vmem((edges, n * halo), BF16),
        vmem((edges, nodes), BF16),
        vmem((nodes, edges), BF16),
        vmem((edges, width), F32),
        vmem((width, edges), BF16),
        vmem((n * halo, width), BF16),
        vmem((edges, width), BF16),
        vmem((nodes, width), F32),
        vmem((nodes, width), BF16),
        vmem((nodes, width), F32),
        vmem((nodes, width), BF16),
        vmem((edges, width), BF16),
        vmem((bands // 2, share, width), BF16),
        vmem((3, doms, doms * doms, share // 3, cols), BF16),
        vmem((3, doms - 1, doms * doms, share // 3, cols), BF16),
        vmem((3, doms * doms, share // 3, cols), BF16),
        vmem((3, doms * doms, share // 3, cols), BF16),
        vmem((n * cap, grid), BF16),
    ]
    dma = pltpu.SemaphoreType.DMA
    for _ in range(2):
        scratch += [dma, dma((CHUNKS,))]
    scratch += [dma] * 6 + [dma, dma((3,)), dma, dma]
    operands = (
        grid_inputs.T,
        mesh_latent,
        edge_state,
        cotangent.T,
        w_embed,
        w_send,
        w_recv,
        w_edge,
        w_mesh_out,
        w_grid_out,
        w_predict.T,
        enc_owner.reshape(1, grid),
        enc_local.reshape(1, grid),
        halo_rows[0].T,
        edge_src_dev.reshape(1, edges),
        edge_src_slot.reshape(1, edges),
        edge_dst.reshape(1, edges),
    )
    scratch = [vmem(a.shape, a.dtype) for a in operands] + [pltpu.SemaphoreType.DMA((INPUTS,))] + scratch
    prediction, gradient = pl.pallas_call(
        functools.partial(kernel, side, side, doms, cap, halo),
        out_shape=(
            jax.ShapeDtypeStruct((outs, grid), BF16),
            jax.ShapeDtypeStruct((share, cols), F32),
        ),
        in_specs=[pl.BlockSpec(memory_space=pl.ANY)] * INPUTS,
        out_specs=(pl.BlockSpec(memory_space=vmem),) * 2,
        scratch_shapes=scratch,
        compiler_params=pltpu.CompilerParams(
            collective_id=0, has_side_effects=True, vmem_limit_bytes=63 * 1024 * 1024
        ),
        cost_estimate=pl.CostEstimate(flops=25 * 10**9, bytes_accessed=10**7, transcendentals=10**7),
    )(*operands)
    results = (prediction, gradient)
    prediction, gradient = pl.pallas_call(
        hand_over,
        out_shape=tuple(jax.ShapeDtypeStruct(a.shape, a.dtype) for a in results),
        in_specs=[pl.BlockSpec(memory_space=vmem)] * 2,
        out_specs=(pl.BlockSpec(memory_space=vmem),) * 2,
    )(*results)
    return prediction.T, gradient


def solution(mesh):
    both = ("band", "dom")
    return jax.shard_map(
        functools.partial(body, bands=mesh.shape["band"], doms=mesh.shape["dom"]),
        mesh=mesh,
        in_specs=(P(both, None),) * 4
        + (P(),) * 7
        + (P(both, None), P(both), P(both, None, None), P(both), P(both), P(both)),
        out_specs=(P(both, None), P("band", "dom")),
        check_vma=False,
    )
```

```python
import functools

import jax
import jax.numpy as jnp
from jax import lax
from jax.experimental import pallas as pl
from jax.experimental.pallas import tpu as pltpu
from jax.sharding import PartitionSpec as P

MESH = pl.DeviceIdType.MESH
F32 = jnp.float32
BF16 = jnp.bfloat16
CHUNKS = 8
AHEAD = 4
INPUTS = 17
STRIDE = 53
STRIDE_INVERSE = 29


def sigmoid(value):
    return 0.5 * jnp.tanh(0.5 * value) + 0.5


def dot(a, b):
    return jnp.dot(a, b, preferred_element_type=F32)


def dot_t(a, b):
    return lax.dot_general(a, b, (((1,), (1,)), ((), ())), preferred_element_type=F32)


def one_hot(mask):
    return jnp.where(mask, 1.0, 0.0).astype(BF16)


def iota(shape, dim):
    return lax.broadcasted_iota(jnp.int32, shape, dim)


def column(row):
    wide = jnp.broadcast_to(row.astype(F32), (8, row.shape[1]))
    return jnp.transpose(wide)[:, :1].astype(jnp.int32)


def moments(values):
    center = values - jnp.mean(values, axis=-1, keepdims=True)
    spread = jnp.mean(center * center, axis=-1, keepdims=True)
    scale = lax.rsqrt(spread + 1e-05)
    return center * scale, scale


def fold(values, parts, depth):
    half = values.shape[1] // 2
    cut = values.reshape(parts, depth, 2 * half)
    return jnp.concatenate([cut[:, :, :half], cut[:, :, half:]], axis=1).astype(BF16)


def unfold(values):
    parts, twice, half = values.shape
    depth = twice // 2
    wide = values.astype(F32)
    return jnp.concatenate([wide[:, :depth], wide[:, depth:]], axis=2).reshape(parts * depth, 2 * half)


def kernel(
    nx,
    nz,
    ny,
    cap,
    halo,
    *refs,
):
    inputs, refs = refs[:INPUTS], refs[INPUTS:]
    pred_ref, grad_ref, *refs = refs
    held, loaded, refs = refs[:INPUTS], refs[INPUTS], refs[INPUTS + 1 :]
    (
        x_ref,
        ml_ref,
        es_ref,
        cot_ref,
        wemb_ref,
        wsend_ref,
        wrecv_ref,
        wedge_ref,
        wm_ref,
        wg_ref,
        wp_ref,
        owner_ref,
        local_ref,
        halo_ref,
        dev_ref,
        slot_ref,
        dst_ref,
    ) = held
    (
        xs,
        cs,
        web,
        wpp,
        wpt,
        slots,
        sbuf,
        rbuf,
        csbuf,
        crbuf,
        obuf,
        inbuf,
        bsend,
        bland,
        hbuf,
        own,
        ownt,
        query,
        agg,
        enc,
        hal,
        osnd,
        orcv,
        orcvt,
        part,
        est,
        inb,
        snd,
        esum,
        mesh_part,
        dz,
        dsum,
        dpre,
        gland,
        line1,
        land1,
        line2,
        land2,
        pick,
        a_send,
        a_recv,
        c_send,
        c_recv,
        h_send,
        h_recv,
        b_send,
        b_recv,
        p_send,
        p_recv,
        q_send,
        q_recv,
        g_send,
        g_recv,
    ) = refs
    n = nx * nz * 2 * ny
    width_in, grid = x_ref.shape
    nodes, width = ml_ref.shape
    edges = es_ref.shape[0]
    outs = cot_ref.shape[0]
    spc = n // CHUNKS
    rows = spc * cap
    epc = edges // CHUNKS
    band, y = lax.axis_index("band"), lax.axis_index("dom")
    k = lax.rem(band, 2)
    me = band * ny + y

    def shift(r, sign):
        to = lax.rem(me + r * (STRIDE if sign > 0 else n - STRIDE % n), n)
        return lax.div(to, ny), lax.rem(to, ny)

    barrier = pltpu.get_barrier_semaphore()

    def greet(r, carry):
        pl.semaphore_signal(barrier, inc=1, device_id=shift(r, 1), device_id_type=MESH)
        return carry

    lax.fori_loop(1, n, greet, 0)

    order = (11, 12, 0, 3, 1, 4, 6, 16, 14, 15, 2, 7, 13, 10, 5, 9, 8)
    for i in order:
        pltpu.make_async_copy(inputs[i], held[i], loaded.at[i]).start()

    def ready(*which):
        for i in which:
            pltpu.make_async_copy(inputs[i], held[i], loaded.at[i]).wait()

    ready(11, 12)
    o = owner_ref[...]
    member = jnp.where(o == iota((n, grid), 0), 1.0, 0.0)
    tri = min(128, grid)
    before = one_hot(iota((tri, tri), 0) < iota((tri, tri), 1))
    base = jnp.zeros((n, 1), F32)
    ranks = []
    for i in range(grid // tri):
        m = member[:, i * tri : (i + 1) * tri]
        count = dot(m.astype(BF16), before) + base
        ranks.append(jnp.sum(count * m, axis=0, keepdims=True))
        base = base + jnp.sum(m, axis=1, keepdims=True)
    rank = jnp.concatenate(ranks, axis=1).astype(jnp.int32)
    slots[...] = (((o - me) * STRIDE_INVERSE) & (n - 1)) * cap + rank

    ready(0, 3)
    first = width_in // 16 * 16
    xs[first:, :] = jnp.zeros((width - first, grid), BF16)
    xs[:width_in, :] = x_ref[...]
    tail = xs[first : first + 16, :].astype(F32)
    mark = iota((16, grid), 0) == width_in - first
    xs[first : first + 16, :] = jnp.where(mark, (local_ref[...] + 1).astype(F32), tail).astype(BF16)
    first = outs // 16 * 16
    cs[first:, :] = jnp.zeros((cs.shape[0] - first, grid), BF16)
    cs[:outs, :] = cot_ref[...]

    def send(src, dst, send_sem, recv_sem, to):
        pltpu.make_async_remote_copy(
            src_ref=src, dst_ref=dst, send_sem=send_sem, recv_sem=recv_sem, device_id=to, device_id_type=MESH
        ).start()

    def take(ref, sem):
        pltpu.make_async_copy(ref, ref, sem).wait()

    def send_parts(c, src, dst, send_sem, recv_sem, sign):
        def one(i, carry):
            r = c * spc + i

            @pl.when(r > 0)
            def _():
                send(src.at[r], dst.at[r], send_sem, recv_sem.at[c], shift(r, sign))

            return carry

        lax.fori_loop(0, spc, one, 0, unroll=4)

        @pl.when(c == 0)
        def _():
            pltpu.make_async_copy(src.at[0], dst.at[0], recv_sem.at[0]).start()

    def pack(c, carry):
        place = one_hot(slots[...] == iota((rows, grid), 0) + c * rows)
        pick[pl.ds(pl.multiple_of(c * rows, rows), rows), :] = place
        sbuf[pl.ds(c * spc, spc)] = fold(dot_t(place, xs[...]), spc, cap)
        csbuf[pl.ds(c * spc, spc)] = fold(dot_t(place, cs[...]), spc, cap)
        return carry

    def pack_and_send(c, carry):
        pack(c, carry)
        return send_rows(c, carry)

    def send_rows(c, carry):
        send_parts(c, sbuf, rbuf, a_send, a_recv, 1)
        return carry

    lax.fori_loop(0, AHEAD, pack, 0)
    pl.semaphore_wait(barrier, n - 1)
    lax.fori_loop(0, AHEAD, send_rows, 0)
    lax.fori_loop(AHEAD, CHUNKS, pack_and_send, 0)

    def send_cot(c, carry):
        send_parts(c, csbuf, crbuf, c_send, c_recv, 1)
        return carry

    ready(1, 4, 6, 16, 14, 15, 2, 7, 13, 10, 5, 9, 8)
    first = width_in // 16 * 16
    web[first:, :] = jnp.zeros((width - first, width), BF16)
    web[:width_in, :] = wemb_ref[...]
    first = outs // 16 * 16
    wpt[first:, :] = jnp.zeros((wpt.shape[0] - first, width), BF16)
    wpt[:outs, :] = wp_ref[...]
    wpp[...] = jnp.transpose(wpt[...])
    halo_col = jnp.transpose(halo_ref[...].astype(F32)).astype(BF16)
    query[...] = dot(ml_ref[...], wrecv_ref[...]).astype(BF16)

    def encode(c, carry):
        take(rbuf.at[pl.ds(c * spc, spc)], a_recv.at[c])
        wide = unfold(rbuf[pl.ds(c * spc, spc)])
        mark = iota((rows, 128), 1) == width_in - (width - 128)
        label = jnp.sum(jnp.where(mark, wide[:, width - 128 :], 0.0), axis=1, keepdims=True)
        hit = one_hot(label.astype(jnp.int32) - 1 == iota((rows, nodes), 1))
        lines = pl.ds(pl.multiple_of(c * rows, rows), rows)
        own[lines, :] = hit
        hit_t = jnp.transpose(hit)
        ownt[:, lines] = hit_t
        hid = dot(wide.astype(BF16), web[...])
        hid = (hid * sigmoid(hid)).astype(BF16)
        hbuf[lines, :] = hid
        arg = dot(hid, wsend_ref[...]) + dot(hit, query[...])
        agg[...] += dot(hit_t, (arg * sigmoid(arg)).astype(BF16))
        return carry

    def prepare(c, carry):
        lines = pl.ds(pl.multiple_of(c * epc, epc), epc)
        dst = dst_ref[:, lines]
        orcvt[:, lines] = one_hot(dst == iota((nodes, epc), 0))
        orcv[lines, :] = one_hot(column(dst) == iota((epc, nodes), 1))
        source = column(dev_ref[:, lines] * halo + slot_ref[:, lines])
        osnd[lines, :] = one_hot(source == iota((epc, n * halo), 1))
        state = es_ref[lines, :]
        est[:, lines] = jnp.transpose(state)
        part[lines, :] = dot(state, wedge_ref[:width, :])
        hpc = n * halo // CHUNKS
        spots = pl.ds(pl.multiple_of(c * hpc, hpc), hpc)
        to = (me + (iota((hpc, n), 0) + c * hpc) // halo * STRIDE) & (n - 1)
        spread = one_hot(to == iota((hpc, n), 1))
        label = jnp.where(iota((hpc, halo), 0) % halo == iota((hpc, halo), 1), dot(spread, halo_col), 0.0)
        label = jnp.sum(label, axis=1, keepdims=True).astype(jnp.int32)
        hal[spots, :] = one_hot(label == iota((hpc, nodes), 1))
        return carry

    lax.fori_loop(0, CHUNKS, prepare, 0)
    agg[...] = jnp.zeros_like(agg)
    lax.fori_loop(0, CHUNKS, encode, 0)

    encoded = (ml_ref[...].astype(F32) + moments(agg[...])[0]).astype(BF16)
    enc[...] = encoded

    def outbound(c, carry):
        hpc = n * halo // CHUNKS
        spots = pl.ds(pl.multiple_of(c * hpc, hpc), hpc)
        obuf[pl.ds(c * spc, spc)] = fold(dot(hal[spots, :], enc[...]), spc, halo)

        def one(i, inner):
            r = c * spc + i

            @pl.when(r > 0)
            def _():
                send(obuf.at[r], inbuf.at[me], h_send, h_recv, shift(r, 1))

            return inner

        lax.fori_loop(0, spc, one, 0, unroll=4)
        return carry

    lax.fori_loop(0, CHUNKS, outbound, 0)
    pltpu.make_async_copy(obuf.at[0], inbuf.at[me], h_recv).start()
    lax.fori_loop(0, CHUNKS, send_cot, 0)

    own_part = dot(enc[...], wedge_ref[2 * width :, :]).astype(BF16)
    mesh_part[...] = own_part

    def edge_own(c, carry):
        lines = pl.ds(pl.multiple_of(c * epc, epc), epc)
        part[lines, :] += dot(orcv[lines, :], mesh_part[...])
        return carry

    lax.fori_loop(0, CHUNKS, edge_own, 0)
    esum[...] = jnp.zeros_like(esum)
    take(inbuf, h_recv)
    inb[...] = unfold(inbuf[...]).astype(BF16)

    def edge_forward(c, carry):
        lines = pl.ds(pl.multiple_of(c * epc, epc), epc)
        sender = dot(osnd[lines, :], inb[...]).astype(BF16)
        snd[lines, :] = sender
        pre = part[lines, :] + dot(sender, wedge_ref[width : 2 * width, :])
        part[lines, :] = pre
        esum[...] += dot(orcvt[:, lines], (pre * sigmoid(pre)).astype(BF16))
        return carry

    lax.fori_loop(0, CHUNKS, edge_forward, 0)
    normed, scale = moments(esum[...])
    updated = (enc[...].astype(F32) + normed).astype(BF16)
    mesh_part[...] = dot(updated, wm_ref[...]).astype(BF16)
    dz[...] = jnp.zeros_like(dz)

    def decode(c, carry):
        lines = pl.ds(pl.multiple_of(c * rows, rows), rows)
        zed = dot(hbuf[lines, :], wg_ref[...]) + dot(own[lines, :], mesh_part[...])
        sig = sigmoid(zed)
        bsend[pl.ds(c * spc, spc)] = fold(dot((zed * sig).astype(BF16), wpp[...]), spc, cap)

        def one(i, inner):
            r = c * spc + i

            @pl.when(r > 0)
            def _():
                send(bsend.at[r], bland.at[r], b_send, b_recv, shift(r, -1))

            return inner

        lax.fori_loop(0, spc, one, 0, unroll=4)
        take(crbuf.at[pl.ds(c * spc, spc)], c_recv.at[c])
        slope = dot(unfold(crbuf[pl.ds(c * spc, spc)]).astype(BF16), wpt[...])
        slope = (slope * sig * (1.0 + zed * (1.0 - sig))).astype(BF16)
        dz[...] += dot(ownt[:, lines], slope)
        return carry

    lax.fori_loop(0, CHUNKS, decode, 0)
    pltpu.make_async_copy(bsend.at[0], bland.at[0], b_recv).start()

    slope = lax.dot_general(
        dz[...].astype(BF16), wm_ref[...], (((1,), (1,)), ((), ())), preferred_element_type=F32
    )
    normed, scale = moments(esum[...])
    slope = scale * (
        slope
        - jnp.mean(slope, axis=-1, keepdims=True)
        - normed * jnp.mean(slope * normed, axis=-1, keepdims=True)
    )
    dsum[...] = slope.astype(BF16)

    def edge_backward(c, carry):
        lines = pl.ds(pl.multiple_of(c * epc, epc), epc)
        pre = part[lines, :]
        sig = sigmoid(pre)
        slope = dot(orcv[lines, :], dsum[...])
        dpre[lines, :] = (slope * sig * (1.0 + pre * (1.0 - sig))).astype(BF16)
        return carry

    lax.fori_loop(0, CHUNKS, edge_backward, 0)
    share = 3 * width // (nx * nz * 2)

    def send_pair(i, carry):
        block = pl.ds(pl.multiple_of((i * 2 + 1 - k) * share, 16), share)
        send(hbuf.at[block, :], gland.at[i], p_send, p_recv, (band + 1 - 2 * k, y))
        return carry

    hbuf[:width, :] = dot(est[...], dpre[...]).astype(BF16)
    cut = width // (2 * share)
    lax.fori_loop(0, cut, send_pair, 0)
    hbuf[width : 2 * width, :] = lax.dot_general(
        snd[...], dpre[...], (((0,), (0,)), ((), ())), preferred_element_type=F32
    ).astype(BF16)
    cut, done = 2 * width // (2 * share), cut
    lax.fori_loop(done, cut, send_pair, 0)
    received = dot(orcvt[...], dpre[...]).astype(BF16)
    hbuf[2 * width : 3 * width, :] = lax.dot_general(
        enc[...], received, (((0,), (0,)), ((), ())), preferred_element_type=F32
    ).astype(BF16)
    lax.fori_loop(cut, nx * nz, send_pair, 0)
    take(gland, p_recv)
    cols = width // ny
    third = share // 3
    place3 = (lax.div(band, 2 * nz), lax.rem(lax.div(band, 2), nz), y)

    def add_pair(i, carry):
        block = pl.ds(pl.multiple_of((i * 2 + k) * share, 16), share)
        both = (hbuf[block, :].astype(F32) + gland[i].astype(F32)).astype(BF16)
        tx, tz = lax.div(i, nz), lax.rem(i, nz)
        for d in range(ny):
            part3 = both[:, d * cols : (d + 1) * cols]
            line1[0, tx, tz * ny + d] = part3[:third]
            line1[1, tz, tx * ny + d] = part3[third : 2 * third]
            line1[2, d, i] = part3[2 * third :]
        return carry

    lax.fori_loop(0, nx * nz, add_pair, 0)

    def device(axis, along, rest):
        two = [lax.div(rest, ny), lax.rem(rest, ny)]
        tx, tz, ty = two[:axis] + [along] + two[axis:]
        return (tx * nz + tz) * 2 + k, ty

    def others(axis):
        a, b = place3[:axis] + place3[axis + 1 :]
        return a * ny + b

    for step in range(1, ny):
        for axis in range(3):
            to = lax.rem(place3[axis] + step, ny)
            send(
                line1.at[axis, to], land1.at[axis, step - 1], q_send, q_recv.at[axis], device(axis, to, others(axis))
            )
    for axis in range(3):
        take(land1.at[axis], q_recv.at[axis])
        total = line1[axis, place3[axis]].astype(F32)
        for step in range(1, ny):
            total += land1[axis, step - 1].astype(F32)
        line2[axis] = total.astype(BF16)
        mine = others(axis)

        def send_line(r, carry, axis=axis, mine=mine):
            to = lax.rem(mine + r * 5, ny * ny)
            send(line2.at[axis, to], land2.at[axis, mine], g_send, g_recv, device(axis, place3[axis], to))
            return carry

        lax.fori_loop(1, ny * ny, send_line, 0)
        pltpu.make_async_copy(line2.at[axis, mine], land2.at[axis, mine], g_recv).start()

    take(bland, b_recv)

    def arrange(c, carry):
        lines = pl.ds(pl.multiple_of(c * rows, rows), rows)
        ownt[:, lines] = jnp.transpose(unfold(bland[pl.ds(c * spc, spc)]).astype(BF16))
        return carry

    lax.fori_loop(0, CHUNKS, arrange, 0)
    gpc = min(256, grid)

    def choose(c, carry):
        spots = pl.ds(pl.multiple_of(c * gpc, gpc), gpc)
        pred_ref[:, spots] = dot(ownt[...], pick[:, spots])[:outs].astype(BF16)
        return carry

    lax.fori_loop(0, grid // gpc, choose, 0)
    take(land2, g_recv)
    for axis in range(3):
        grad_ref[axis * third : (axis + 1) * third, :] = jnp.sum(land2[axis].astype(F32), axis=0)
    take(sbuf.at[pl.ds(1, n - 1)], a_send)
    take(csbuf.at[pl.ds(1, n - 1)], c_send)
    take(obuf.at[pl.ds(1, n - 1)], h_send)
    take(bsend.at[pl.ds(1, n - 1)], b_send)
    take(gland, p_send)
    take(land1, q_send)
    take(land2.at[:, pl.ds(1, ny * ny - 1)], g_send)


def hand_over(pred_ref, grad_ref, pred_out, grad_out):
    pred_out[...] = pred_ref[...]
    grad_out[...] = grad_ref[...]


def body(
    grid_inputs,
    mesh_latent,
    edge_state,
    cotangent,
    w_embed,
    w_send,
    w_recv,
    w_edge,
    w_mesh_out,
    w_grid_out,
    w_predict,
    enc_owner,
    enc_local,
    halo_rows,
    edge_src_dev,
    edge_src_slot,
    edge_dst,
    bands,
    doms,
):
    side = int(round((bands // 2) ** 0.5))
    n = bands * doms
    grid = grid_inputs.shape[0]
    nodes, width = mesh_latent.shape
    edges = edge_state.shape[0]
    outs = cotangent.shape[1]
    wide_out = 256
    cap = 3 * grid // n
    halo = halo_rows.shape[2]
    share, cols = 3 * width // bands, width // doms
    vmem = pltpu.VMEM
    scratch = [
        vmem((width, grid), BF16),
        vmem((wide_out, grid), BF16),
        vmem((width, width), BF16),
        vmem((width, wide_out), BF16),
        vmem((wide_out, width), BF16),
        vmem((1, grid), jnp.int32),
        vmem((n, 2 * cap, width // 2), BF16),
        vmem((n, 2 * cap, width // 2), BF16),
        vmem((n, 2 * cap, wide_out // 2), BF16),
        vmem((n, 2 * cap, wide_out // 2), BF16),
        vmem((n, 2 * halo, width // 2), BF16),
        vmem((n, 2 * halo, width // 2), BF16),
        vmem((n, 2 * cap, wide_out // 2), BF16),
        vmem((n, 2 * cap, wide_out // 2), BF16),
        vmem((max(n * cap, 3 * width), width), BF16),
        vmem((n * cap, nodes), BF16),
        vmem((nodes, n * cap), BF16),
        vmem((nodes, width), BF16),
        vmem((nodes, width), F32),
        vmem((nodes, width), BF16),
        vmem((n * halo, nodes), BF16),
        vmem((edges, n * halo), BF16),
        vmem((edges, nodes), BF16),
        vmem((nodes, edges), BF16),
        vmem((edges, width), F32),
        vmem((width, edges), BF16),
        vmem((n * halo, width), BF16),
        vmem((edges, width), BF16),
        vmem((nodes, width), F32),
        vmem((nodes, width), BF16),
        vmem((nodes, width), F32),
        vmem((nodes, width), BF16),
        vmem((edges, width), BF16),
        vmem((bands // 2, share, width), BF16),
        vmem((3, doms, doms * doms, share // 3, cols), BF16),
        vmem((3, doms - 1, doms * doms, share // 3, cols), BF16),
        vmem((3, doms * doms, share // 3, cols), BF16),
        vmem((3, doms * doms, share // 3, cols), BF16),
        vmem((n * cap, grid), BF16),
    ]
    dma = pltpu.SemaphoreType.DMA
    for _ in range(2):
        scratch += [dma, dma((CHUNKS,))]
    scratch += [dma] * 6 + [dma, dma((3,)), dma, dma]
    operands = (
        grid_inputs.T,
        mesh_latent,
        edge_state,
        cotangent.T,
        w_embed,
        w_send,
        w_recv,
        w_edge,
        w_mesh_out,
        w_grid_out,
        w_predict.T,
        enc_owner.reshape(1, grid),
        enc_local.reshape(1, grid),
        halo_rows[0].T,
        edge_src_dev.reshape(1, edges),
        edge_src_slot.reshape(1, edges),
        edge_dst.reshape(1, edges),
    )
    scratch = [vmem(a.shape, a.dtype) for a in operands] + [pltpu.SemaphoreType.DMA((INPUTS,))] + scratch
    prediction, gradient = pl.pallas_call(
        functools.partial(kernel, side, side, doms, cap, halo),
        out_shape=(
            jax.ShapeDtypeStruct((outs, grid), BF16),
            jax.ShapeDtypeStruct((share, cols), F32),
        ),
        in_specs=[pl.BlockSpec(memory_space=pl.ANY)] * INPUTS,
        out_specs=(pl.BlockSpec(memory_space=vmem),) * 2,
        scratch_shapes=scratch,
        compiler_params=pltpu.CompilerParams(
            collective_id=0, has_side_effects=True, vmem_limit_bytes=63 * 1024 * 1024
        ),
        cost_estimate=pl.CostEstimate(flops=25 * 10**9, bytes_accessed=10**7, transcendentals=10**7),
    )(*operands)
    results = (prediction, gradient)
    prediction, gradient = pl.pallas_call(
        hand_over,
        out_shape=tuple(jax.ShapeDtypeStruct(a.shape, a.dtype) for a in results),
        in_specs=[pl.BlockSpec(memory_space=vmem)] * 2,
        out_specs=(pl.BlockSpec(memory_space=vmem),) * 2,
    )(*results)
    return prediction.T, gradient


def solution(mesh):
    both = ("band", "dom")
    return jax.shard_map(
        functools.partial(body, bands=mesh.shape["band"], doms=mesh.shape["dom"]),
        mesh=mesh,
        in_specs=(P(both, None),) * 4
        + (P(),) * 7
        + (P(both, None), P(both), P(both, None, None), P(both), P(both), P(both)),
        out_specs=(P(both, None), P("band", "dom")),
        check_vma=False,
    )
```

```python
import functools

import jax
import jax.numpy as jnp
from jax import lax
from jax.experimental import pallas as pl
from jax.experimental.pallas import tpu as pltpu
from jax.sharding import PartitionSpec as P

MESH = pl.DeviceIdType.MESH
F32 = jnp.float32
BF16 = jnp.bfloat16
CHUNKS = 8
AHEAD = 4
INPUTS = 17
STRIDE = 53
STRIDE_INVERSE = 29


def sigmoid(value):
    return 0.5 * jnp.tanh(0.5 * value) + 0.5


def dot(a, b):
    return jnp.dot(a, b, preferred_element_type=F32)


def dot_t(a, b):
    return lax.dot_general(a, b, (((1,), (1,)), ((), ())), preferred_element_type=F32)


def one_hot(mask):
    return jnp.where(mask, 1.0, 0.0).astype(BF16)


def iota(shape, dim):
    return lax.broadcasted_iota(jnp.int32, shape, dim)


def column(row):
    wide = jnp.broadcast_to(row.astype(F32), (8, row.shape[1]))
    return jnp.transpose(wide)[:, :1].astype(jnp.int32)


def moments(values):
    center = values - jnp.mean(values, axis=-1, keepdims=True)
    spread = jnp.mean(center * center, axis=-1, keepdims=True)
    scale = lax.rsqrt(spread + 1e-05)
    return center * scale, scale


def fold(values, parts, depth):
    half = values.shape[1] // 2
    cut = values.reshape(parts, depth, 2 * half)
    return jnp.concatenate([cut[:, :, :half], cut[:, :, half:]], axis=1).astype(BF16)


def unfold(values):
    parts, twice, half = values.shape
    depth = twice // 2
    wide = values.astype(F32)
    return jnp.concatenate([wide[:, :depth], wide[:, depth:]], axis=2).reshape(parts * depth, 2 * half)


def kernel(
    nx,
    nz,
    ny,
    cap,
    halo,
    *refs,
):
    inputs, refs = refs[:INPUTS], refs[INPUTS:]
    pred_ref, grad_ref, *refs = refs
    held, loaded, refs = refs[:INPUTS], refs[INPUTS], refs[INPUTS + 1 :]
    (
        x_ref,
        ml_ref,
        es_ref,
        cot_ref,
        wemb_ref,
        wsend_ref,
        wrecv_ref,
        wedge_ref,
        wm_ref,
        wg_ref,
        wp_ref,
        owner_ref,
        local_ref,
        halo_ref,
        dev_ref,
        slot_ref,
        dst_ref,
    ) = held
    (
        xs,
        cs,
        web,
        wpp,
        wpt,
        slots,
        sbuf,
        rbuf,
        csbuf,
        crbuf,
        obuf,
        inbuf,
        bsend,
        bland,
        hbuf,
        own,
        ownt,
        query,
        agg,
        enc,
        hal,
        osnd,
        orcv,
        orcvt,
        part,
        est,
        inb,
        snd,
        esum,
        mesh_part,
        dz,
        dsum,
        dpre,
        gland,
        line1,
        land1,
        line2,
        land2,
        pick,
        a_send,
        a_recv,
        c_send,
        c_recv,
        h_send,
        h_recv,
        b_send,
        b_recv,
        p_send,
        p_recv,
        q_send,
        q_recv,
        g_send,
        g_recv,
    ) = refs
    n = nx * nz * 2 * ny
    width_in, grid = x_ref.shape
    nodes, width = ml_ref.shape
    edges = es_ref.shape[0]
    outs = cot_ref.shape[0]
    spc = n // CHUNKS
    rows = spc * cap
    epc = edges // CHUNKS
    band, y = lax.axis_index("band"), lax.axis_index("dom")
    k = lax.rem(band, 2)
    me = band * ny + y

    def shift(r, sign):
        to = lax.rem(me + r * (STRIDE if sign > 0 else n - STRIDE % n), n)
        return lax.div(to, ny), lax.rem(to, ny)

    barrier = pltpu.get_barrier_semaphore()

    def greet(r, carry):
        pl.semaphore_signal(barrier, inc=1, device_id=shift(r, 1), device_id_type=MESH)
        return carry

    lax.fori_loop(1, n, greet, 0)

    order = (11, 12, 0, 3, 1, 4, 6, 16, 14, 15, 2, 7, 13, 10, 5, 9, 8)
    for i in order:
        pltpu.make_async_copy(inputs[i], held[i], loaded.at[i]).start()

    def ready(*which):
        for i in which:
            pltpu.make_async_copy(inputs[i], held[i], loaded.at[i]).wait()

    ready(11, 12)
    o = owner_ref[...]
    member = jnp.where(o == iota((n, grid), 0), 1.0, 0.0)
    tri = min(128, grid)
    before = one_hot(iota((tri, tri), 0) < iota((tri, tri), 1))
    base = jnp.zeros((n, 1), F32)
    ranks = []
    for i in range(grid // tri):
        m = member[:, i * tri : (i + 1) * tri]
        count = dot(m.astype(BF16), before) + base
        ranks.append(jnp.sum(count * m, axis=0, keepdims=True))
        base = base + jnp.sum(m, axis=1, keepdims=True)
    rank = jnp.concatenate(ranks, axis=1).astype(jnp.int32)
    slots[...] = (((o - me) * STRIDE_INVERSE) & (n - 1)) * cap + rank

    ready(0, 3)
    first = width_in // 16 * 16
    xs[first:, :] = jnp.zeros((width - first, grid), BF16)
    xs[:width_in, :] = x_ref[...]
    tail = xs[first : first + 16, :].astype(F32)
    mark = iota((16, grid), 0) == width_in - first
    xs[first : first + 16, :] = jnp.where(mark, (local_ref[...] + 1).astype(F32), tail).astype(BF16)
    first = outs // 16 * 16
    cs[first:, :] = jnp.zeros((cs.shape[0] - first, grid), BF16)
    cs[:outs, :] = cot_ref[...]

    def send(src, dst, send_sem, recv_sem, to):
        pltpu.make_async_remote_copy(
            src_ref=src, dst_ref=dst, send_sem=send_sem, recv_sem=recv_sem, device_id=to, device_id_type=MESH
        ).start()

    def take(ref, sem):
        pltpu.make_async_copy(ref, ref, sem).wait()

    def send_parts(c, src, dst, send_sem, recv_sem, sign):
        def one(i, carry):
            r = c * spc + i

            @pl.when(r > 0)
            def _():
                send(src.at[r], dst.at[r], send_sem, recv_sem.at[c], shift(r, sign))

            return carry

        lax.fori_loop(0, spc, one, 0, unroll=4)

        @pl.when(c == 0)
        def _():
            pltpu.make_async_copy(src.at[0], dst.at[0], recv_sem.at[0]).start()

    def pack(c, carry):
        place = one_hot(slots[...] == iota((rows, grid), 0) + c * rows)
        pick[pl.ds(pl.multiple_of(c * rows, rows), rows), :] = place
        sbuf[pl.ds(c * spc, spc)] = fold(dot_t(place, xs[...]), spc, cap)
        return carry

    def pack_and_send(c, carry):
        pack(c, carry)
        return send_rows(c, carry)

    def send_rows(c, carry):
        send_parts(c, sbuf, rbuf, a_send, a_recv, 1)
        return carry

    lax.fori_loop(0, AHEAD, pack, 0)
    pl.semaphore_wait(barrier, n - 1)
    lax.fori_loop(0, AHEAD, send_rows, 0)
    lax.fori_loop(AHEAD, CHUNKS, pack_and_send, 0)

    def pack_cot(c, carry):
        place = pick[pl.ds(pl.multiple_of(c * rows, rows), rows), :]
        csbuf[pl.ds(c * spc, spc)] = fold(dot_t(place, cs[...]), spc, cap)
        return carry

    lax.fori_loop(0, CHUNKS, pack_cot, 0)

    def send_cot(c, carry):
        send_parts(c, csbuf, crbuf, c_send, c_recv, 1)
        return carry

    ready(1, 4, 6, 16, 14, 15, 2, 7, 13, 10, 5, 9, 8)
    first = width_in // 16 * 16
    web[first:, :] = jnp.zeros((width - first, width), BF16)
    web[:width_in, :] = wemb_ref[...]
    first = outs // 16 * 16
    wpt[first:, :] = jnp.zeros((wpt.shape[0] - first, width), BF16)
    wpt[:outs, :] = wp_ref[...]
    wpp[...] = jnp.transpose(wpt[...])
    halo_col = jnp.transpose(halo_ref[...].astype(F32)).astype(BF16)
    query[...] = dot(ml_ref[...], wrecv_ref[...]).astype(BF16)

    def encode(c, carry):
        take(rbuf.at[pl.ds(c * spc, spc)], a_recv.at[c])
        wide = unfold(rbuf[pl.ds(c * spc, spc)])
        mark = iota((rows, 128), 1) == width_in - (width - 128)
        label = jnp.sum(jnp.where(mark, wide[:, width - 128 :], 0.0), axis=1, keepdims=True)
        hit = one_hot(label.astype(jnp.int32) - 1 == iota((rows, nodes), 1))
        lines = pl.ds(pl.multiple_of(c * rows, rows), rows)
        own[lines, :] = hit
        hit_t = jnp.transpose(hit)
        ownt[:, lines] = hit_t
        hid = dot(wide.astype(BF16), web[...])
        hid = (hid * sigmoid(hid)).astype(BF16)
        hbuf[lines, :] = hid
        arg = dot(hid, wsend_ref[...]) + dot(hit, query[...])
        agg[...] += dot(hit_t, (arg * sigmoid(arg)).astype(BF16))
        return carry

    def prepare(c, carry):
        lines = pl.ds(pl.multiple_of(c * epc, epc), epc)
        dst = dst_ref[:, lines]
        orcvt[:, lines] = one_hot(dst == iota((nodes, epc), 0))
        orcv[lines, :] = one_hot(column(dst) == iota((epc, nodes), 1))
        source = column(dev_ref[:, lines] * halo + slot_ref[:, lines])
        osnd[lines, :] = one_hot(source == iota((epc, n * halo), 1))
        state = es_ref[lines, :]
        est[:, lines] = jnp.transpose(state)
        part[lines, :] = dot(state, wedge_ref[:width, :])
        hpc = n * halo // CHUNKS
        spots = pl.ds(pl.multiple_of(c * hpc, hpc), hpc)
        to = (me + (iota((hpc, n), 0) + c * hpc) // halo * STRIDE) & (n - 1)
        spread = one_hot(to == iota((hpc, n), 1))
        label = jnp.where(iota((hpc, halo), 0) % halo == iota((hpc, halo), 1), dot(spread, halo_col), 0.0)
        label = jnp.sum(label, axis=1, keepdims=True).astype(jnp.int32)
        hal[spots, :] = one_hot(label == iota((hpc, nodes), 1))
        return carry

    lax.fori_loop(0, CHUNKS, prepare, 0)
    agg[...] = jnp.zeros_like(agg)
    lax.fori_loop(0, CHUNKS, encode, 0)

    encoded = (ml_ref[...].astype(F32) + moments(agg[...])[0]).astype(BF16)
    enc[...] = encoded

    def outbound(c, carry):
        hpc = n * halo // CHUNKS
        spots = pl.ds(pl.multiple_of(c * hpc, hpc), hpc)
        obuf[pl.ds(c * spc, spc)] = fold(dot(hal[spots, :], enc[...]), spc, halo)

        def one(i, inner):
            r = c * spc + i

            @pl.when(r > 0)
            def _():
                send(obuf.at[r], inbuf.at[me], h_send, h_recv, shift(r, 1))

            return inner

        lax.fori_loop(0, spc, one, 0, unroll=4)
        return carry

    lax.fori_loop(0, CHUNKS, outbound, 0)
    pltpu.make_async_copy(obuf.at[0], inbuf.at[me], h_recv).start()
    lax.fori_loop(0, CHUNKS, send_cot, 0)

    own_part = dot(enc[...], wedge_ref[2 * width :, :]).astype(BF16)
    mesh_part[...] = own_part

    def edge_own(c, carry):
        lines = pl.ds(pl.multiple_of(c * epc, epc), epc)
        part[lines, :] += dot(orcv[lines, :], mesh_part[...])
        return carry

    lax.fori_loop(0, CHUNKS, edge_own, 0)
    esum[...] = jnp.zeros_like(esum)
    take(inbuf, h_recv)
    inb[...] = unfold(inbuf[...]).astype(BF16)

    def edge_forward(c, carry):
        lines = pl.ds(pl.multiple_of(c * epc, epc), epc)
        sender = dot(osnd[lines, :], inb[...]).astype(BF16)
        snd[lines, :] = sender
        pre = part[lines, :] + dot(sender, wedge_ref[width : 2 * width, :])
        part[lines, :] = pre
        esum[...] += dot(orcvt[:, lines], (pre * sigmoid(pre)).astype(BF16))
        return carry

    lax.fori_loop(0, CHUNKS, edge_forward, 0)
    normed, scale = moments(esum[...])
    updated = (enc[...].astype(F32) + normed).astype(BF16)
    mesh_part[...] = dot(updated, wm_ref[...]).astype(BF16)
    dz[...] = jnp.zeros_like(dz)

    def decode(c, carry):
        lines = pl.ds(pl.multiple_of(c * rows, rows), rows)
        zed = dot(hbuf[lines, :], wg_ref[...]) + dot(own[lines, :], mesh_part[...])
        sig = sigmoid(zed)
        bsend[pl.ds(c * spc, spc)] = fold(dot((zed * sig).astype(BF16), wpp[...]), spc, cap)

        def one(i, inner):
            r = c * spc + i

            @pl.when(r > 0)
            def _():
                send(bsend.at[r], bland.at[r], b_send, b_recv, shift(r, -1))

            return inner

        lax.fori_loop(0, spc, one, 0, unroll=4)
        take(crbuf.at[pl.ds(c * spc, spc)], c_recv.at[c])
        slope = dot(unfold(crbuf[pl.ds(c * spc, spc)]).astype(BF16), wpt[...])
        slope = (slope * sig * (1.0 + zed * (1.0 - sig))).astype(BF16)
        dz[...] += dot(ownt[:, lines], slope)
        return carry

    lax.fori_loop(0, CHUNKS, decode, 0)
    pltpu.make_async_copy(bsend.at[0], bland.at[0], b_recv).start()

    slope = lax.dot_general(
        dz[...].astype(BF16), wm_ref[...], (((1,), (1,)), ((), ())), preferred_element_type=F32
    )
    normed, scale = moments(esum[...])
    slope = scale * (
        slope
        - jnp.mean(slope, axis=-1, keepdims=True)
        - normed * jnp.mean(slope * normed, axis=-1, keepdims=True)
    )
    dsum[...] = slope.astype(BF16)

    def edge_backward(c, carry):
        lines = pl.ds(pl.multiple_of(c * epc, epc), epc)
        pre = part[lines, :]
        sig = sigmoid(pre)
        slope = dot(orcv[lines, :], dsum[...])
        dpre[lines, :] = (slope * sig * (1.0 + pre * (1.0 - sig))).astype(BF16)
        return carry

    lax.fori_loop(0, CHUNKS, edge_backward, 0)
    share = 3 * width // (nx * nz * 2)

    def send_pair(i, carry):
        block = pl.ds(pl.multiple_of((i * 2 + 1 - k) * share, 16), share)
        send(hbuf.at[block, :], gland.at[i], p_send, p_recv, (band + 1 - 2 * k, y))
        return carry

    hbuf[:width, :] = dot(est[...], dpre[...]).astype(BF16)
    cut = width // (2 * share)
    lax.fori_loop(0, cut, send_pair, 0)
    hbuf[width : 2 * width, :] = lax.dot_general(
        snd[...], dpre[...], (((0,), (0,)), ((), ())), preferred_element_type=F32
    ).astype(BF16)
    cut, done = 2 * width // (2 * share), cut
    lax.fori_loop(done, cut, send_pair, 0)
    received = dot(orcvt[...], dpre[...]).astype(BF16)
    hbuf[2 * width : 3 * width, :] = lax.dot_general(
        enc[...], received, (((0,), (0,)), ((), ())), preferred_element_type=F32
    ).astype(BF16)
    lax.fori_loop(cut, nx * nz, send_pair, 0)
    take(gland, p_recv)
    cols = width // ny
    third = share // 3
    place3 = (lax.div(band, 2 * nz), lax.rem(lax.div(band, 2), nz), y)

    def add_pair(i, carry):
        block = pl.ds(pl.multiple_of((i * 2 + k) * share, 16), share)
        both = (hbuf[block, :].astype(F32) + gland[i].astype(F32)).astype(BF16)
        tx, tz = lax.div(i, nz), lax.rem(i, nz)
        for d in range(ny):
            part3 = both[:, d * cols : (d + 1) * cols]
            line1[0, tx, tz * ny + d] = part3[:third]
            line1[1, tz, tx * ny + d] = part3[third : 2 * third]
            line1[2, d, i] = part3[2 * third :]
        return carry

    lax.fori_loop(0, nx * nz, add_pair, 0)

    def device(axis, along, rest):
        two = [lax.div(rest, ny), lax.rem(rest, ny)]
        tx, tz, ty = two[:axis] + [along] + two[axis:]
        return (tx * nz + tz) * 2 + k, ty

    def others(axis):
        a, b = place3[:axis] + place3[axis + 1 :]
        return a * ny + b

    for step in range(1, ny):
        for axis in range(3):
            to = lax.rem(place3[axis] + step, ny)
            send(
                line1.at[axis, to], land1.at[axis, step - 1], q_send, q_recv.at[axis], device(axis, to, others(axis))
            )
    for axis in range(3):
        take(land1.at[axis], q_recv.at[axis])
        total = line1[axis, place3[axis]].astype(F32)
        for step in range(1, ny):
            total += land1[axis, step - 1].astype(F32)
        line2[axis] = total.astype(BF16)
        mine = others(axis)

        def send_line(r, carry, axis=axis, mine=mine):
            to = lax.rem(mine + r * 5, ny * ny)
            send(line2.at[axis, to], land2.at[axis, mine], g_send, g_recv, device(axis, place3[axis], to))
            return carry

        lax.fori_loop(1, ny * ny, send_line, 0)
        pltpu.make_async_copy(line2.at[axis, mine], land2.at[axis, mine], g_recv).start()

    take(bland, b_recv)

    def arrange(c, carry):
        lines = pl.ds(pl.multiple_of(c * rows, rows), rows)
        ownt[:, lines] = jnp.transpose(unfold(bland[pl.ds(c * spc, spc)]).astype(BF16))
        return carry

    lax.fori_loop(0, CHUNKS, arrange, 0)
    gpc = min(256, grid)

    def choose(c, carry):
        spots = pl.ds(pl.multiple_of(c * gpc, gpc), gpc)
        pred_ref[:, spots] = dot(ownt[...], pick[:, spots])[:outs].astype(BF16)
        return carry

    lax.fori_loop(0, grid // gpc, choose, 0)
    take(land2, g_recv)
    for axis in range(3):
        grad_ref[axis * third : (axis + 1) * third, :] = jnp.sum(land2[axis].astype(F32), axis=0)
    take(sbuf.at[pl.ds(1, n - 1)], a_send)
    take(csbuf.at[pl.ds(1, n - 1)], c_send)
    take(obuf.at[pl.ds(1, n - 1)], h_send)
    take(bsend.at[pl.ds(1, n - 1)], b_send)
    take(gland, p_send)
    take(land1, q_send)
    take(land2.at[:, pl.ds(1, ny * ny - 1)], g_send)


def hand_over(pred_ref, grad_ref, pred_out, grad_out):
    pred_out[...] = pred_ref[...]
    grad_out[...] = grad_ref[...]


def body(
    grid_inputs,
    mesh_latent,
    edge_state,
    cotangent,
    w_embed,
    w_send,
    w_recv,
    w_edge,
    w_mesh_out,
    w_grid_out,
    w_predict,
    enc_owner,
    enc_local,
    halo_rows,
    edge_src_dev,
    edge_src_slot,
    edge_dst,
    bands,
    doms,
):
    side = int(round((bands // 2) ** 0.5))
    n = bands * doms
    grid = grid_inputs.shape[0]
    nodes, width = mesh_latent.shape
    edges = edge_state.shape[0]
    outs = cotangent.shape[1]
    wide_out = 256
    cap = 3 * grid // n
    halo = halo_rows.shape[2]
    share, cols = 3 * width // bands, width // doms
    vmem = pltpu.VMEM
    scratch = [
        vmem((width, grid), BF16),
        vmem((wide_out, grid), BF16),
        vmem((width, width), BF16),
        vmem((width, wide_out), BF16),
        vmem((wide_out, width), BF16),
        vmem((1, grid), jnp.int32),
        vmem((n, 2 * cap, width // 2), BF16),
        vmem((n, 2 * cap, width // 2), BF16),
        vmem((n, 2 * cap, wide_out // 2), BF16),
        vmem((n, 2 * cap, wide_out // 2), BF16),
        vmem((n, 2 * halo, width // 2), BF16),
        vmem((n, 2 * halo, width // 2), BF16),
        vmem((n, 2 * cap, wide_out // 2), BF16),
        vmem((n, 2 * cap, wide_out // 2), BF16),
        vmem((max(n * cap, 3 * width), width), BF16),
        vmem((n * cap, nodes), BF16),
        vmem((nodes, n * cap), BF16),
        vmem((nodes, width), BF16),
        vmem((nodes, width), F32),
        vmem((nodes, width), BF16),
        vmem((n * halo, nodes), BF16),
        vmem((edges, n * halo), BF16),
        vmem((edges, nodes), BF16),
        vmem((nodes, edges), BF16),
        vmem((edges, width), F32),
        vmem((width, edges), BF16),
        vmem((n * halo, width), BF16),
        vmem((edges, width), BF16),
        vmem((nodes, width), F32),
        vmem((nodes, width), BF16),
        vmem((nodes, width), F32),
        vmem((nodes, width), BF16),
        vmem((edges, width), BF16),
        vmem((bands // 2, share, width), BF16),
        vmem((3, doms, doms * doms, share // 3, cols), BF16),
        vmem((3, doms - 1, doms * doms, share // 3, cols), BF16),
        vmem((3, doms * doms, share // 3, cols), BF16),
        vmem((3, doms * doms, share // 3, cols), BF16),
        vmem((n * cap, grid), BF16),
    ]
    dma = pltpu.SemaphoreType.DMA
    for _ in range(2):
        scratch += [dma, dma((CHUNKS,))]
    scratch += [dma] * 6 + [dma, dma((3,)), dma, dma]
    operands = (
        grid_inputs.T,
        mesh_latent,
        edge_state,
        cotangent.T,
        w_embed,
        w_send,
        w_recv,
        w_edge,
        w_mesh_out,
        w_grid_out,
        w_predict.T,
        enc_owner.reshape(1, grid),
        enc_local.reshape(1, grid),
        halo_rows[0].T,
        edge_src_dev.reshape(1, edges),
        edge_src_slot.reshape(1, edges),
        edge_dst.reshape(1, edges),
    )
    scratch = [vmem(a.shape, a.dtype) for a in operands] + [pltpu.SemaphoreType.DMA((INPUTS,))] + scratch
    prediction, gradient = pl.pallas_call(
        functools.partial(kernel, side, side, doms, cap, halo),
        out_shape=(
            jax.ShapeDtypeStruct((outs, grid), BF16),
            jax.ShapeDtypeStruct((share, cols), F32),
        ),
        in_specs=[pl.BlockSpec(memory_space=pl.ANY)] * INPUTS,
        out_specs=(pl.BlockSpec(memory_space=vmem),) * 2,
        scratch_shapes=scratch,
        compiler_params=pltpu.CompilerParams(
            collective_id=0, has_side_effects=True, vmem_limit_bytes=63 * 1024 * 1024
        ),
        cost_estimate=pl.CostEstimate(flops=25 * 10**9, bytes_accessed=10**7, transcendentals=10**7),
    )(*operands)
    results = (prediction, gradient)
    prediction, gradient = pl.pallas_call(
        hand_over,
        out_shape=tuple(jax.ShapeDtypeStruct(a.shape, a.dtype) for a in results),
        in_specs=[pl.BlockSpec(memory_space=vmem)] * 2,
        out_specs=(pl.BlockSpec(memory_space=vmem),) * 2,
    )(*results)
    return prediction.T, gradient


def solution(mesh):
    both = ("band", "dom")
    return jax.shard_map(
        functools.partial(body, bands=mesh.shape["band"], doms=mesh.shape["dom"]),
        mesh=mesh,
        in_specs=(P(both, None),) * 4
        + (P(),) * 7
        + (P(both, None), P(both), P(both, None, None), P(both), P(both), P(both)),
        out_specs=(P(both, None), P("band", "dom")),
        check_vma=False,
    )
```
